256 devices in a mesh: expert: 64 (over x, z_lo, y, core), dp: 4 (over z_hi).
Axes of the slice: x: 4, y: 4, z: 8 (z_hi: 4, z_lo: 2; z = z_hi * 2 + z_lo), core: 2. Of those that a mesh axis runs over, the one named last changes fastest.
Arguments:
- tokens: bfloat16 [32768, 3584], P(('expert', 'dp')), may hold values from -6 to 6
- cotangent: bfloat16 [32768, 3584], P(('expert', 'dp')), may hold values from -0.29882812 to 0.29882812
- routes: int32 [32768, 2], P(('expert', 'dp')), may hold values from 0 to 63, as said below
- gates: float32 [32768, 2], P(('expert', 'dp')), may hold values from 0.1 to 1
- gate_weight: bfloat16 [64, 3584, 1024], P('expert'), may hold values from -0.09375 to 0.09375
Outputs:
- grad_down: float32 [64, 1024, 3584], P('expert', 'dp')
The draws below stay inside these ranges and needn't reach their ends.
Inputs may be any that keep to these rules, and one draw needn't show every extreme that they name: `routes`: one expert, the same for all devices, is named exactly 12 times in the rows of each device; every other expert is named at most 6 times in the rows of one device, and some expert exactly 6 times; the 2 experts of a row differ.
All inputs are finite; a program needn't handle non-finite values.
Results may differ from the reference program's by a relative error of at most 0.004.
Values may be sent and summed in bfloat16 or wider, within the bound.
No kernel may reach another device: no remote copies, remote signals or barrier semaphores. Data moves between devices by JAX's collectives and lax.ppermute only.
A program may use at most 128 MiB of HBM per device.

```python
import jax
import jax.numpy as jnp
from jax import lax

D = 3584
H = 1024
TOP = 2
TOK_DEV = 128
EXPERTS = 64
CAP = 6
HOT_LOAD = 12
TOKENS = 32768


def draw_routes(key, part):
    key = jax.random.fold_in(key, 11)
    hottest = jax.random.randint(jax.random.fold_in(key, 0), (), 0, EXPERTS).astype(jnp.int32)
    blocks = TOKENS // TOK_DEV
    cold_list = ((hottest + 1 + jnp.arange(EXPERTS - 1, dtype=jnp.int32)) % EXPERTS).astype(jnp.int32)
    pool = jnp.repeat(cold_list, CAP)
    pool_size = (EXPERTS - 1) * CAP
    cold_slots = TOK_DEV * TOP - HOT_LOAD

    def one_block(block_key):
        first_key, second_key, third_key = jax.random.split(block_key, 3)
        chosen = cold_list[jax.random.randint(first_key, (), 0, EXPERTS - 1)]
        scores = jax.random.randint(second_key, (pool_size,), 0, 1 << 20)
        scores = jnp.where(pool == chosen, -1, scores) * pool_size + jnp.arange(pool_size, dtype=jnp.int32)
        picked = jnp.argsort(scores)
        taken = pool[picked[:cold_slots]].astype(jnp.int32)
        hot_part = jnp.full((HOT_LOAD,), hottest, jnp.int32)
        sequence = jnp.sort(jnp.concatenate([hot_part, taken]))
        table = sequence.reshape(TOP, TOK_DEV).T
        return table[jax.random.permutation(third_key, TOK_DEV)]
    block_keys = jax.random.split(jax.random.fold_in(key, 1), blocks)
    return jax.vmap(one_block)(block_keys).reshape(TOKENS, TOP).astype(jnp.int32)


def level_of(own_key, dims, cuts, low, high):
    def one(dim, blocks):
        steps = jax.random.uniform(jax.random.fold_in(jax.random.fold_in(own_key, 6), dim), (blocks,), jnp.float32, low / len(cuts), high / len(cuts))
        return jnp.repeat(jnp.exp(steps), dims[dim] // blocks).reshape((-1,) + (1,) * (len(dims) - dim - 1))

    factor_of = one(*cuts[0])
    for cut in cuts[1:]:
        factor_of = factor_of * one(*cut)
    return factor_of


def noise(own_key, shape, deviation, reach, cuts=(), held_as=jnp.bfloat16):
    result = jax.random.normal(own_key, shape, jnp.float32) * deviation
    if len(cuts) > 0:
        result = level_of(own_key, shape, cuts, -0.22, 0.18) * result
    return jnp.clip(result, min=-reach, max=reach).astype(held_as)


def setup_inputs(seed: int = 0) -> dict:
    keys = jax.random.split(jax.random.key(seed), 6)
    tokens = noise(keys[0], (TOKENS, D), 1.0, 6.0, ((0, 256),))
    cotangent = noise(keys[1], (TOKENS, D), 0.05, 0.29882812, ((0, 256),))
    routes = draw_routes(jax.random.fold_in(keys[5], 71), 0)
    gates = jnp.clip(0.1 + 0.9 * jax.random.uniform(keys[3], (TOKENS, TOP), jnp.float32) ** level_of(keys[3], (TOKENS, TOP), ((0, 256),), -0.2, 0.2), 0.1, 1.0)
    gate_weight = noise(keys[4], (EXPERTS, D, H), D ** -0.5, 0.09375, ((0, 64),))
    return {"tokens": tokens, "cotangent": cotangent, "routes": routes, "gates": gates, "gate_weight": gate_weight}


def reference(tokens, cotangent, routes, gates, gate_weight):
    tile = 512
    flat = routes.reshape(-1).astype(jnp.int32)
    total = flat.shape[0]
    order = jnp.argsort(flat, stable=True).astype(jnp.int32)
    counts = jnp.sum((flat[:, None] == jnp.arange(EXPERTS, dtype=jnp.int32)[None, :]).astype(jnp.int32), 0)
    offsets = (jnp.cumsum(counts) - counts).astype(jnp.int32)
    tiles_each = (counts + tile - 1) // tile
    tile_first = (jnp.cumsum(tiles_each) - tiles_each).astype(jnp.int32)
    n_tiles = total // tile + EXPERTS
    flat_gates = gates.reshape(-1)

    def step(grad, index):
        expert = (jnp.sum((tile_first <= index).astype(jnp.int32)) - 1).astype(jnp.int32)
        local = index - tile_first[expert]
        position = local * tile + jnp.arange(tile, dtype=jnp.int32)
        valid = position < counts[expert]
        where_sorted = jnp.where(valid, offsets[expert] + position, 0).astype(jnp.int32)
        route = order[where_sorted]
        token = (route // TOP).astype(jnp.int32)
        token_rows = tokens[token]
        gate_rows = flat_gates[route]
        scaled_rows = (gate_rows[:, None] * cotangent[token].astype(jnp.float32)).astype(jnp.bfloat16)
        weight = gate_weight[expert]
        hidden = jax.nn.silu(jnp.dot(token_rows, weight, preferred_element_type=jnp.float32))
        hidden = jnp.where(valid[:, None], hidden, jnp.zeros_like(hidden)).astype(jnp.bfloat16)
        partial_term = lax.dot_general(hidden, scaled_rows, (((0,), (0,)), ((), ())), preferred_element_type=jnp.float32)
        grad = grad.at[expert].add(partial_term)
        return grad, None

    start_grad = jnp.zeros((EXPERTS, H, D), jnp.float32)
    grad, _ = lax.scan(step, start_grad, jnp.arange(n_tiles, dtype=jnp.int32))
    return grad
```

```python
import functools

import jax
import jax.numpy as jnp
from jax import lax
from jax.experimental import pallas as pl
from jax.experimental.pallas import tpu as pltpu
from jax.sharding import PartitionSpec as P

CAP = 6
F32 = jnp.float32
BF16 = jnp.bfloat16
VMEM_LIMIT = 56 * 1024 * 1024


def iota(shape, dim):
    return lax.broadcasted_iota(jnp.int32, shape, dim)


def floordiv(a, n):
    return jnp.floor((a.astype(F32) + 0.5) * (1.0 / n)).astype(jnp.int32)


def slot_keys(route, experts):
    tok = route.shape[1]
    column = route.T
    r0, r1 = route[0:1], route[1:2]
    c0, c1 = column[:, 0:1], column[:, 1:2]
    before = iota((tok, tok), 0) < iota((tok, tok), 1)

    def count(mask):
        return jnp.sum(jnp.where(mask, 1.0, 0.0), 0, keepdims=True)

    rank0 = count((c0 == r0) & before)
    rank1 = count(c0 == r1) + count((c1 == r1) & before)

    def key(r, rank):
        return jnp.where(rank < CAP, r * CAP + rank, experts * CAP + rank - CAP).astype(jnp.int32)

    return key(r0, rank0), key(r1, rank1)


def pack_tokens_kernel(experts, route_ref, head_ref, tail_ref, out_ref):
    k = pl.program_id(0)
    key0, key1 = slot_keys(route_ref[...], experts)
    rows = out_ref.shape[0]
    row = iota((rows, 1), 0)
    e, j = row >> 4, row & 15
    base = jnp.where(j < 8, e * CAP, experts * CAP)
    jj = j & 7
    head_slot = jnp.where(jj < CAP, base + jj, -1)
    tail_slot = jnp.where(jj >= CAP, base + 2 * k + jj - CAP, -1)

    def pick(slot):
        return jnp.where((slot == key0) | (slot == key1), 1.0, 0.0).astype(BF16)

    left = jnp.concatenate([pick(head_slot), pick(tail_slot)], 1)
    right = jnp.concatenate([head_ref[...], tail_ref[...]], 0)
    out_ref[...] = jnp.dot(left, right, preferred_element_type=F32).astype(BF16)


def pack_tokens(route, tokens, experts):
    tok, width = tokens.shape
    part = width // 4
    rows = experts * 16
    return pl.pallas_call(
        functools.partial(pack_tokens_kernel, experts),
        grid=(3,),
        in_specs=[
            pl.BlockSpec(route.shape, lambda k: (0, 0)),
            pl.BlockSpec((tok, part), lambda k: (0, k)),
            pl.BlockSpec((tok, part), lambda k: (0, 3)),
        ],
        out_specs=pl.BlockSpec((rows, part), lambda k: (0, k)),
        out_shape=jax.ShapeDtypeStruct((rows, 3 * part), BF16),
        compiler_params=pltpu.CompilerParams(vmem_limit_bytes=VMEM_LIMIT),
        name="pack_tokens",
    )(route, tokens, tokens)


def pack_scaled_kernel(experts, dests, raw_ref, out_ref):
    planes, _, part = raw_ref.shape
    tok = 128
    span = planes * CAP
    rows = dests * 2 * span
    row = iota((rows, 1), 0)
    e = floordiv(row, 2 * span)
    j = row - e * (2 * span)
    e = e + pl.program_id(0) * dests
    extra = j >= span
    j = jnp.where(extra, j - span, j)
    plane = floordiv(j, CAP)
    s = j - plane * CAP
    slot = jnp.where(extra, experts * CAP + s, e * CAP + s)
    lefts, rights = [], []
    gate = jnp.zeros((rows, 1), F32)
    for p in range(planes):
        meta = raw_ref[p, tok : tok + 16, 0:tok].astype(F32)
        key0, key1 = slot_keys(meta[0:8], experts)
        gate0 = (meta[2:3] + meta[3:4]) + meta[4:5]
        gate1 = (meta[5:6] + meta[6:7]) + meta[7:8]
        mine = jnp.where(plane == p, slot, -1)
        hit0, hit1 = mine == key0, mine == key1
        both = jnp.where(hit0, gate0, 0.0) + jnp.where(hit1, gate1, 0.0)
        gate = gate + jnp.sum(both, 1, keepdims=True)
        lefts.append(jnp.where(hit0 | hit1, 1.0, 0.0).astype(BF16))
        rights.append(raw_ref[p, 0:tok, :])
    left, right = jnp.concatenate(lefts, 1), jnp.concatenate(rights, 0)
    rows_out = jnp.dot(left, right, preferred_element_type=F32)
    out_ref[...] = (gate * rows_out).astype(BF16)


def pack_scaled(raw, experts):
    planes, _, part = raw.shape
    dests = 8
    rows = dests * 2 * planes * CAP
    return pl.pallas_call(
        functools.partial(pack_scaled_kernel, experts, dests),
        grid=(experts // dests,),
        in_specs=[pl.BlockSpec(raw.shape, lambda g: (0, 0, 0))],
        out_specs=pl.BlockSpec((rows, part), lambda g: (g, 0)),
        out_shape=jax.ShapeDtypeStruct((experts * 2 * planes * CAP, part), BF16),
        compiler_params=pltpu.CompilerParams(vmem_limit_bytes=VMEM_LIMIT),
        name="pack_scaled",
    )(raw)


def hidden_kernel(hot_ref, x_ref, w_ref, main_ref, extra_ref, rows_ref):
    sources, _, _, head = x_ref.shape
    part = head // 3
    half = sources // 2
    is_hot = hot_ref[0] > 0
    count = sources * CAP

    def unfold(which):
        r = iota((half * CAP, half * 8), 0)
        c = iota((half * CAP, half * 8), 1)
        src = floordiv(r, CAP)
        s = r - src * CAP

        def pick(mask):
            return jnp.where(mask, 1.0, 0.0).astype(BF16)

        for h in range(2):
            x = x_ref[h * half : (h + 1) * half, which].reshape(half * 8, head)
            rows = pl.ds(which * count + h * half * CAP, half * CAP)
            rows_ref[rows, 0:head] = jnp.dot(
                pick(c == src * 8 + s), x, preferred_element_type=F32
            ).astype(BF16)
            tail = jnp.zeros((half * CAP, part), F32)
            for k in range(3):
                mask = (c == src * 8 + CAP + s - 2 * k) & (s >= 2 * k) & (s < 2 * k + 2)
                tail = tail + jnp.dot(
                    pick(mask), x[:, k * part : (k + 1) * part], preferred_element_type=F32
                )
            rows_ref[rows, head:] = tail.astype(BF16)

    @pl.when(pl.program_id(0) == 0)
    def _():
        unfold(0)

        @pl.when(is_hot)
        def _():
            unfold(1)

    def hidden(first):
        v = jnp.dot(rows_ref[first : first + count, :], w_ref[...], preferred_element_type=F32)
        return (v / (1.0 + jnp.exp(-v))).astype(BF16)

    main_ref[...] = hidden(0)

    @pl.when(is_hot)
    def _():
        extra_ref[...] = hidden(count)

    @pl.when(jnp.logical_not(is_hot))
    def _():
        extra_ref[...] = jnp.zeros_like(extra_ref)


def hidden_of(hot, x, weight):
    sources, _, _, head = x.shape
    width, hid = weight.shape
    count = sources * CAP
    block = 256
    return pl.pallas_call(
        hidden_kernel,
        grid=(hid // block,),
        in_specs=[
            pl.BlockSpec(memory_space=pltpu.SMEM),
            pl.BlockSpec(x.shape, lambda n: (0, 0, 0, 0)),
            pl.BlockSpec((width, block), lambda n: (0, n)),
        ],
        out_specs=[pl.BlockSpec((count, block), lambda n: (0, n))] * 2,
        out_shape=[jax.ShapeDtypeStruct((count, hid), BF16)] * 2,
        scratch_shapes=[pltpu.VMEM((2 * count, width), BF16)],
        compiler_params=pltpu.CompilerParams(vmem_limit_bytes=VMEM_LIMIT),
        name="hidden_of",
    )(hot, x, weight)


def grad_kernel(group, hot_ref, main_ref, extra_ref, s_ref, out_ref, acc_ref):
    planes, _, hid = main_ref.shape
    part = s_ref.shape[-1]
    g = pl.program_id(0)
    n = group * CAP
    rows = planes * n

    o, i = iota((rows, rows), 0), iota((rows, rows), 1)
    plane = floordiv(o, n)
    rest = o - plane * n
    src = floordiv(rest, CAP)
    perm = jnp.where(i == src * planes * CAP + plane * CAP + rest - src * CAP, 1.0, 0.0).astype(BF16)

    def term(h_ref, which):
        s = s_ref[:, which].reshape(rows, part)
        s = jnp.dot(perm, s, preferred_element_type=F32).astype(BF16)
        h = h_ref[...].reshape(rows, hid)
        return lax.dot_general(h, s, (((0,), (0,)), ((), ())), preferred_element_type=F32)

    @pl.when(g == 0)
    def _():
        acc_ref[...] = term(main_ref, 0)

    @pl.when(g > 0)
    def _():
        acc_ref[...] += term(main_ref, 0)

    @pl.when(hot_ref[0] > 0)
    def _():
        acc_ref[...] += term(extra_ref, 1)

    @pl.when(g == pl.num_programs(0) - 1)
    def _():
        out_ref[...] = acc_ref[...].astype(out_ref.dtype)


def grad_of(hot, main, extra, s):
    planes, count, hid = main.shape
    sources, _, span, part = s.shape
    group = 16
    h_spec = pl.BlockSpec((planes, group * CAP, hid), lambda g: (0, g, 0))
    return pl.pallas_call(
        functools.partial(grad_kernel, group),
        grid=(sources // group,),
        in_specs=[
            pl.BlockSpec(memory_space=pltpu.SMEM),
            h_spec,
            h_spec,
            pl.BlockSpec((group, 2, span, part), lambda g: (g, 0, 0, 0)),
        ],
        out_specs=pl.BlockSpec((hid, part), lambda g: (0, 0)),
        out_shape=jax.ShapeDtypeStruct((hid, part), BF16),
        scratch_shapes=[pltpu.VMEM((hid, part), F32)],
        compiler_params=pltpu.CompilerParams(vmem_limit_bytes=VMEM_LIMIT),
        name="grad_of",
    )(hot, main, extra, s)


def bf16_parts(x):
    high = lax.reduce_precision(x, 8, 7)
    mid = lax.reduce_precision(x - high, 8, 7)
    return [high, mid, x - high - mid]


def gather_planes(x):
    planes = lax.axis_size("dp")
    me = lax.axis_index("dp")
    got = [x] + [
        lax.ppermute(x, "dp", [((i + d) % planes, i) for i in range(planes)]) for d in range(1, planes)
    ]
    stacked = jnp.stack(got)
    return jnp.roll(stacked, me, axis=0)


def local(tokens, cotangent, routes, gates, gate_weight):
    tok, width = tokens.shape
    experts = lax.axis_size("expert")
    planes = lax.axis_size("dp")
    part = width // planes

    route_rows = routes.T.astype(F32)
    gate_rows = gates.T
    meta = jnp.concatenate(
        [route_rows, jnp.stack(bf16_parts(gate_rows[0])), jnp.stack(bf16_parts(gate_rows[1]))], 0
    )
    counts = jnp.sum(
        (routes.reshape(-1)[:, None] == jnp.arange(experts, dtype=jnp.int32)[None, :]).astype(F32), 0
    )
    mine = lax.axis_index("expert")
    hot = (jnp.sum(jnp.where(jnp.arange(experts) == mine, counts, 0.0)) > CAP + 0.5).astype(jnp.int32)
    hot = hot.reshape(1)

    sent = pack_tokens(meta, tokens, experts)
    sent = sent.reshape(experts, 16, 3 * part)
    arrived = lax.all_to_all(sent, "expert", 0, 0, tiled=True)

    meta_block = jnp.pad(meta.astype(BF16), ((0, 8), (0, part - tok)))
    raw = cotangent.reshape(tok, planes, part).transpose(1, 0, 2)
    raw = jnp.concatenate([raw, jnp.broadcast_to(meta_block, (planes, 16, part))], 1)
    raw = lax.all_to_all(raw, "dp", 0, 0, tiled=True)

    scaled = pack_scaled(raw, experts).reshape(experts, 2 * planes * CAP, part)
    scaled = lax.all_to_all(scaled, "expert", 0, 0, tiled=True)

    main, extra = hidden_of(hot, arrived.reshape(experts, 2, 8, 3 * part), gate_weight[0])
    main = lax.all_gather(main, "dp")
    extra = lax.all_gather(extra, "dp")

    grad = grad_of(hot, main, extra, scaled.reshape(experts, 2, planes * CAP, part))
    hid = grad.shape[0] // planes
    grad = lax.all_to_all(grad.reshape(planes, hid, part), "dp", 0, 0, tiled=True)
    return grad.transpose(1, 0, 2).reshape(1, hid, width).astype(F32)


def solution(mesh):
    placed = (
        P(("expert", "dp"), None),
        P(("expert", "dp"), None),
        P(("expert", "dp"), None),
        P(("expert", "dp"), None),
        P("expert", None, None),
    )
    return jax.shard_map(
        local, mesh=mesh, in_specs=placed, out_specs=P("expert", "dp", None), check_vma=False
    )
```

```python
import functools

import jax
import jax.numpy as jnp
from jax import lax
from jax.experimental import pallas as pl
from jax.experimental.pallas import tpu as pltpu
from jax.sharding import PartitionSpec as P

CAP = 6
F32 = jnp.float32
BF16 = jnp.bfloat16
VMEM_LIMIT = 56 * 1024 * 1024


def iota(shape, dim):
    return lax.broadcasted_iota(jnp.int32, shape, dim)


def floordiv(a, n):
    return jnp.floor((a.astype(F32) + 0.5) * (1.0 / n)).astype(jnp.int32)


def slot_keys(route, experts):
    tok = route.shape[1]
    column = route.T
    r0, r1 = route[0:1], route[1:2]
    c0, c1 = column[:, 0:1], column[:, 1:2]
    before = iota((tok, tok), 0) < iota((tok, tok), 1)

    def count(mask):
        return jnp.sum(jnp.where(mask, 1.0, 0.0), 0, keepdims=True)

    rank0 = count((c0 == r0) & before)
    rank1 = count(c0 == r1) + count((c1 == r1) & before)

    def key(r, rank):
        return jnp.where(rank < CAP, r * CAP + rank, experts * CAP + rank - CAP).astype(jnp.int32)

    return key(r0, rank0), key(r1, rank1)


def split_raw_kernel(place_ref, q0_ref, q1_ref, q2_ref, q3_ref, meta_ref, *out_refs):
    tok = q0_ref.shape[0]
    note = jnp.concatenate([meta_ref[...], jnp.zeros_like(meta_ref)], 0).astype(BF16)
    for in_ref, out_ref in zip((q0_ref, q1_ref, q2_ref, q3_ref), out_refs):
        out_ref[0:tok, :] = in_ref[...]
        out_ref[tok:, :] = jnp.zeros((16, in_ref.shape[1]), BF16)
        out_ref[tok:, 0:tok] = note


def split_raw(place, cotangent, meta):
    tok, width = cotangent.shape
    part = width // 4
    quarter = [pl.BlockSpec((tok, part), lambda i, s, d=d: (0, lax.rem(s[1] + d, 4))) for d in range(4)]
    return pl.pallas_call(
        split_raw_kernel,
        grid_spec=pltpu.PrefetchScalarGridSpec(
            num_scalar_prefetch=1,
            grid=(1,),
            in_specs=quarter + [pl.BlockSpec(meta.shape, lambda i, s: (0, 0))],
            out_specs=[pl.BlockSpec((tok + 16, part), lambda i, s: (0, 0))] * 4,
        ),
        out_shape=[jax.ShapeDtypeStruct((tok + 16, part), BF16)] * 4,
        compiler_params=pltpu.CompilerParams(vmem_limit_bytes=VMEM_LIMIT),
        name="split_raw",
    )(place, cotangent, cotangent, cotangent, cotangent, meta)


def pick(mask):
    return jnp.where(mask, 1.0, 0.0).astype(BF16)


def expert_of(dest, z):
    return (dest >> 3) * 16 + z * 8 + (dest & 7)


def pack_tokens_kernel(experts, place_ref, a_meta, b_meta, a_head, b_head, a_tail, b_tail, out_ref):
    k = pl.program_id(0)
    dests, _, _, part = out_ref.shape
    keys = [slot_keys(m[...], experts) for m in (a_meta, b_meta)]
    right = jnp.concatenate([a_head[...], b_head[...], a_tail[...], b_tail[...]], 0)

    def rows_of(rows, base):
        row = iota((rows, 1), 0)
        source, jj = (row >> 3) & 1, row & 7
        parts = []
        for tail in (False, True):
            slot = base + (2 * k + jj - CAP if tail else jj)
            for i, (key0, key1) in enumerate(keys):
                fits = (source == i) & ((jj >= CAP) if tail else (jj < CAP))
                mine = jnp.where(fits, slot, -1)
                parts.append(pick((mine == key0) | (mine == key1)))
        left = jnp.concatenate(parts, 1)
        return jnp.dot(left, right, preferred_element_type=F32).astype(BF16)

    dest = iota((dests * 16, 1), 0) >> 4
    main = rows_of(dests * 16, expert_of(dest, place_ref[3]) * CAP)
    out_ref[:, 0] = main.reshape(dests, 16, part)
    extra = rows_of(16, experts * CAP)
    out_ref[:, 1] = jnp.broadcast_to(extra[None], (dests, 16, part))


def pack_tokens(place, metas, tokens, experts):
    tok, width = tokens[0].shape
    part = width // 4
    dests = experts // 2
    whole = pl.BlockSpec(metas[0].shape, lambda k, s: (0, 0))
    head = pl.BlockSpec((tok, part), lambda k, s: (0, k))
    tail = pl.BlockSpec((tok, part), lambda k, s: (0, 3))
    return pl.pallas_call(
        functools.partial(pack_tokens_kernel, experts),
        grid_spec=pltpu.PrefetchScalarGridSpec(
            num_scalar_prefetch=1,
            grid=(3,),
            in_specs=[whole, whole, head, head, tail, tail],
            out_specs=pl.BlockSpec((dests, 2, 16, part), lambda k, s: (0, 0, 0, k)),
        ),
        out_shape=jax.ShapeDtypeStruct((dests, 2, 16, 3 * part), BF16),
        compiler_params=pltpu.CompilerParams(vmem_limit_bytes=VMEM_LIMIT),
        name="pack_tokens",
    )(place, *metas, *tokens, *tokens)


def pack_scaled_kernel(experts, place_ref, a0, a1, a2, a3, b0, b1, b2, b3, out_ref):
    block, _, _, _, part = out_ref.shape
    tok = 128
    planes = 4
    span = planes * CAP
    first = pl.program_id(0) * block

    for source, raws in enumerate(((a0, a1, a2, a3), (b0, b1, b2, b3))):
        facts = []
        for raw in raws:
            meta = raw[tok : tok + 16, 0:tok].astype(F32)
            gate0 = (meta[2:3] + meta[3:4]) + meta[4:5]
            gate1 = (meta[5:6] + meta[6:7]) + meta[7:8]
            facts.append((*slot_keys(meta[0:8], experts), gate0, gate1))
        right = jnp.concatenate([raw[0:tok, :] for raw in raws], 0)

        def rows_of(slot, plane):
            lefts = []
            gate = jnp.zeros(slot.shape, F32)
            for p, (key0, key1, gate0, gate1) in enumerate(facts):
                mine = jnp.where(plane == p, slot, -1)
                hit0, hit1 = mine == key0, mine == key1
                both = jnp.where(hit0, gate0, 0.0) + jnp.where(hit1, gate1, 0.0)
                gate = gate + jnp.sum(both, 1, keepdims=True)
                lefts.append(pick(hit0 | hit1))
            rows = jnp.dot(jnp.concatenate(lefts, 1), right, preferred_element_type=F32)
            return (gate * rows).astype(BF16)

        row = iota((block * span, 1), 0)
        dest = floordiv(row, span)
        j = row - dest * span
        plane = floordiv(j, CAP)
        slot = expert_of(first + dest, place_ref[3]) * CAP + j - plane * CAP
        out_ref[:, 0, source] = rows_of(slot, plane).reshape(block, span, part)
        j = iota((span, 1), 0)
        plane = floordiv(j, CAP)
        extra = rows_of(experts * CAP + j - plane * CAP, plane)
        out_ref[:, 1, source] = jnp.broadcast_to(extra[None], (block, span, part))


def pack_scaled(place, raws, experts):
    part = raws[0].shape[1]
    dests = experts // 2
    block = 8
    span = 4 * CAP
    return pl.pallas_call(
        functools.partial(pack_scaled_kernel, experts),
        grid_spec=pltpu.PrefetchScalarGridSpec(
            num_scalar_prefetch=1,
            grid=(dests // block,),
            in_specs=[pl.BlockSpec(raws[0].shape, lambda g, s: (0, 0))] * 8,
            out_specs=pl.BlockSpec((block, 2, 2, span, part), lambda g, s: (g, 0, 0, 0, 0)),
        ),
        out_shape=jax.ShapeDtypeStruct((dests, 2, 2, span, part), BF16),
        compiler_params=pltpu.CompilerParams(vmem_limit_bytes=VMEM_LIMIT),
        name="pack_scaled",
    )(place, *raws)


def hidden_kernel(place_ref, x_ref, w_ref, main_ref, extra_ref, rows_ref):
    senders, _, _, head = x_ref.shape
    sources = 2 * senders
    part = head // 3
    half = sources // 2
    is_hot = place_ref[0] > 0
    count = sources * CAP

    def unfold(which):
        r = iota((half * CAP, half * 8), 0)
        c = iota((half * CAP, half * 8), 1)
        src = floordiv(r, CAP)
        s = r - src * CAP
        for h in range(2):
            x = x_ref[h * senders // 2 : (h + 1) * senders // 2, which].reshape(half * 8, head)
            rows = pl.ds(which * count + h * half * CAP, half * CAP)
            rows_ref[rows, 0:head] = jnp.dot(
                pick(c == src * 8 + s), x, preferred_element_type=F32
            ).astype(BF16)
            tail = jnp.zeros((half * CAP, part), F32)
            for k in range(3):
                mask = (c == src * 8 + CAP + s - 2 * k) & (s >= 2 * k) & (s < 2 * k + 2)
                tail = tail + jnp.dot(
                    pick(mask), x[:, k * part : (k + 1) * part], preferred_element_type=F32
                )
            rows_ref[rows, head:] = tail.astype(BF16)

    @pl.when(pl.program_id(0) == 0)
    def _():
        unfold(0)

        @pl.when(is_hot)
        def _():
            unfold(1)

    def hidden(first):
        v = jnp.dot(rows_ref[first : first + count, :], w_ref[...], preferred_element_type=F32)
        return (v / (1.0 + jnp.exp(-v))).astype(BF16)

    main_ref[...] = hidden(0)

    @pl.when(is_hot)
    def _():
        extra_ref[...] = hidden(count)

    @pl.when(jnp.logical_not(is_hot))
    def _():
        extra_ref[...] = jnp.zeros_like(extra_ref)


def hidden_of(place, x, weight):
    senders, _, _, head = x.shape
    width, hid = weight.shape
    count = 2 * senders * CAP
    block = 256
    return pl.pallas_call(
        hidden_kernel,
        grid_spec=pltpu.PrefetchScalarGridSpec(
            num_scalar_prefetch=1,
            grid=(hid // block,),
            in_specs=[
                pl.BlockSpec(x.shape, lambda n, s: (0, 0, 0, 0)),
                pl.BlockSpec((width, block), lambda n, s: (0, n)),
            ],
            out_specs=[pl.BlockSpec((count, block), lambda n, s: (0, n))] * 2,
            scratch_shapes=[pltpu.VMEM((2 * count, width), BF16)],
        ),
        out_shape=[jax.ShapeDtypeStruct((count, hid), BF16)] * 2,
        compiler_params=pltpu.CompilerParams(vmem_limit_bytes=VMEM_LIMIT),
        name="hidden_of",
    )(place, x, weight)


def grad_kernel(place_ref, main_ref, near_ref, far_ref, s_ref, out_ref, acc_ref):
    planes, n, hid = main_ref.shape
    part = s_ref.shape[-1]
    g = pl.program_id(0)
    rows = planes * n

    o, i = iota((rows, rows), 0), iota((rows, rows), 1)
    plane = floordiv(o, n)
    rest = o - plane * n
    src = floordiv(rest, CAP)
    perm = pick(i == src * planes * CAP + plane * CAP + rest - src * CAP)

    def term(h_ref, which):
        s = s_ref[:, which].reshape(rows, part)
        s = jnp.dot(perm, s, preferred_element_type=F32).astype(BF16)
        h = [h_ref[lax.rem(place_ref[1] + planes - d, planes)] for d in range(planes)]
        h = jnp.concatenate(h, 0)
        return lax.dot_general(h, s, (((0,), (0,)), ((), ())), preferred_element_type=F32)

    @pl.when(g == 0)
    def _():
        acc_ref[...] = term(main_ref, 0)

    @pl.when(g > 0)
    def _():
        acc_ref[...] += term(main_ref, 0)

    is_hot = place_ref[0] > 0
    is_near = g // 2 == place_ref[2]

    @pl.when(is_hot & is_near)
    def _():
        acc_ref[...] += term(near_ref, 1)

    @pl.when(is_hot & jnp.logical_not(is_near))
    def _():
        acc_ref[...] += term(far_ref, 1)

    @pl.when(g == pl.num_programs(0) - 1)
    def _():
        out_ref[...] = acc_ref[...].astype(out_ref.dtype)


def grad_of(place, hidden, far, s):
    planes, _, hid = hidden.shape
    senders, _, span, part = s.shape
    group = 8
    block = (planes, 2 * group * CAP, hid)
    return pl.pallas_call(
        grad_kernel,
        grid_spec=pltpu.PrefetchScalarGridSpec(
            num_scalar_prefetch=1,
            grid=(senders // group,),
            in_specs=[
                pl.BlockSpec(block, lambda g, s: (0, g, 0)),
                pl.BlockSpec(block, lambda g, s: (0, 4 + lax.rem(g, 2), 0)),
                pl.BlockSpec(block, lambda g, s: (0, lax.rem(g, 2), 0)),
                pl.BlockSpec((group, 2, span, part), lambda g, s: (g, 0, 0, 0)),
            ],
            out_specs=pl.BlockSpec((hid, part), lambda g, s: (0, 0)),
            scratch_shapes=[pltpu.VMEM((hid, part), F32)],
        ),
        out_shape=jax.ShapeDtypeStruct((hid, part), BF16),
        compiler_params=pltpu.CompilerParams(vmem_limit_bytes=VMEM_LIMIT),
        name="grad_of",
    )(place, hidden, hidden, far, s)


def join_kernel(in_ref, out_ref):
    out_ref[...] = in_ref[...].astype(F32)


def join(parts):
    planes, rows, part = parts.shape
    return pl.pallas_call(
        join_kernel,
        grid=(planes,),
        in_specs=[pl.BlockSpec((1, rows, part), lambda n: (n, 0, 0))],
        out_specs=pl.BlockSpec((1, rows, part), lambda n: (0, 0, n)),
        out_shape=jax.ShapeDtypeStruct((1, rows, planes * part), F32),
        compiler_params=pltpu.CompilerParams(vmem_limit_bytes=VMEM_LIMIT),
        name="join",
    )(parts)


def bf16_parts(x):
    high = lax.reduce_precision(x, 8, 7)
    mid = lax.reduce_precision(x - high, 8, 7)
    return [high, mid, x - high - mid]


def local(tokens, cotangent, routes, gates, gate_weight):
    experts = lax.axis_size("expert")
    planes = lax.axis_size("dp")
    me = lax.axis_index("expert")
    dp = lax.axis_index("dp")
    core = me & 1
    other_z = [(i, i ^ 8) for i in range(experts)]
    other_core = [(i, i ^ 1) for i in range(experts)]
    same_z = [[i for i in range(experts) if (i >> 3) & 1 == z] for z in range(2)]

    route_rows = routes.T.astype(F32)
    gate_rows = gates.T
    meta = jnp.concatenate(
        [route_rows, jnp.stack(bf16_parts(gate_rows[0])), jnp.stack(bf16_parts(gate_rows[1]))], 0
    )
    own = jnp.sum((routes == me).astype(jnp.int32))
    hot = (own > CAP).astype(jnp.int32)
    place = jnp.stack([hot, dp, core, (me >> 3) & 1]).astype(jnp.int32)

    far_tokens = lax.ppermute(tokens, "expert", other_z)
    far_meta = lax.ppermute(meta, "expert", other_z)

    blocks = split_raw(place, cotangent, meta)
    far_tokens, blocks = lax.optimization_barrier((far_tokens, blocks))
    raws = [blocks[0]]
    for d in range(1, planes):
        raws.append(lax.ppermute(blocks[d], "dp", [(i, (i + d) % planes) for i in range(planes)]))
    raws = raws + [lax.ppermute(raw, "expert", other_z) for raw in raws]

    sent = pack_tokens(place, (meta, far_meta), (tokens, far_tokens), experts)
    sent = sent.reshape(experts // 2, 32, sent.shape[-1])
    arrived = lax.all_to_all(sent, "expert", 0, 0, tiled=True, axis_index_groups=same_z)
    arrived = arrived.reshape(experts // 2, 2, 16, arrived.shape[-1])

    scaled = pack_scaled(place, raws, experts)
    span = scaled.shape[-2]
    scaled = scaled.reshape(experts // 2, 4 * span, scaled.shape[-1])
    scaled = lax.all_to_all(scaled, "expert", 0, 0, tiled=True, axis_index_groups=same_z)
    scaled = scaled.reshape(experts // 2, 2, 2 * span, scaled.shape[-1])

    main, extra = hidden_of(place, arrived, gate_weight[0])
    half = extra.shape[0] // 2
    kept = lax.dynamic_slice_in_dim(extra, core * half, half, 0)
    given = lax.dynamic_slice_in_dim(extra, (1 - core) * half, half, 0)
    kept = kept + lax.ppermute(given, "expert", other_core)
    hidden = lax.all_gather(jnp.concatenate([main, kept], 0), "dp")
    far = lax.ppermute(hidden[:, main.shape[0] :], "expert", other_core)

    grad = grad_of(place, hidden, far, scaled)
    hid = grad.shape[0] // planes
    grad = lax.all_to_all(grad.reshape(planes, hid, grad.shape[-1]), "dp", 0, 0, tiled=True)
    return join(grad)


def solution(mesh):
    placed = (
        P(("expert", "dp"), None),
        P(("expert", "dp"), None),
        P(("expert", "dp"), None),
        P(("expert", "dp"), None),
        P("expert", None, None),
    )
    return jax.shard_map(
        local, mesh=mesh, in_specs=placed, out_specs=P("expert", "dp", None), check_vma=False
    )
```

```python
import functools

import jax
import jax.numpy as jnp
from jax import lax
from jax.experimental import pallas as pl
from jax.experimental.pallas import tpu as pltpu
from jax.sharding import PartitionSpec as P

CAP = 6
F32 = jnp.float32
BF16 = jnp.bfloat16
VMEM_LIMIT = 56 * 1024 * 1024


def iota(shape, dim):
    return lax.broadcasted_iota(jnp.int32, shape, dim)


def floordiv(a, n):
    return jnp.floor((a.astype(F32) + 0.5) * (1.0 / n)).astype(jnp.int32)


def slot_keys(route, experts):
    tok = route.shape[1]
    column = route.T
    r0, r1 = route[0:1], route[1:2]
    c0, c1 = column[:, 0:1], column[:, 1:2]
    before = iota((tok, tok), 0) < iota((tok, tok), 1)

    def count(mask):
        return jnp.sum(jnp.where(mask, 1.0, 0.0), 0, keepdims=True)

    rank0 = count((c0 == r0) & before)
    rank1 = count(c0 == r1) + count((c1 == r1) & before)

    def key(r, rank):
        return jnp.where(rank < CAP, r * CAP + rank, experts * CAP + rank - CAP).astype(jnp.int32)

    return key(r0, rank0), key(r1, rank1)


def split_raw_kernel(place_ref, q0_ref, q1_ref, q2_ref, q3_ref, meta_ref, *out_refs):
    tok, part = q0_ref.shape
    note = jnp.concatenate([meta_ref[...], jnp.zeros_like(meta_ref)], 0).astype(BF16)
    note = jnp.concatenate([note, jnp.zeros((16, part - tok), BF16)], 1)
    for in_ref, out_ref in zip((q0_ref, q1_ref, q2_ref, q3_ref), out_refs):
        out_ref[0:tok, :] = in_ref[...]
        out_ref[tok:, :] = note


def split_raw(place, cotangent, meta):
    tok, width = cotangent.shape
    part = width // 4
    quarter = [pl.BlockSpec((tok, part), lambda i, s, d=d: (0, lax.rem(s[1] + d, 4))) for d in range(4)]
    return pl.pallas_call(
        split_raw_kernel,
        grid_spec=pltpu.PrefetchScalarGridSpec(
            num_scalar_prefetch=1,
            grid=(1,),
            in_specs=quarter + [pl.BlockSpec(meta.shape, lambda i, s: (0, 0))],
            out_specs=[pl.BlockSpec((tok + 16, part), lambda i, s: (0, 0))] * 4,
        ),
        out_shape=[jax.ShapeDtypeStruct((tok + 16, part), BF16)] * 4,
        compiler_params=pltpu.CompilerParams(vmem_limit_bytes=VMEM_LIMIT),
        name="split_raw",
    )(place, cotangent, cotangent, cotangent, cotangent, meta)


def pick(mask):
    return jnp.where(mask, 1.0, 0.0).astype(BF16)


def expert_of(dest, z):
    return (dest >> 3) * 16 + z * 8 + (dest & 7)


def fold_rows(place_ref, meta_ref, tokens_ref, out_ref, experts, begin):
    dests = out_ref.shape[0]
    part = tokens_ref.shape[1] // 4
    key0, key1 = slot_keys(meta_ref[...], experts)
    row = iota((dests * 8, 1), 0)
    jj = row & 7
    first = expert_of(row >> 3, place_ref[3]) * CAP

    def choose(slot):
        return pick((slot == key0) | (slot == key1))

    head = choose(jnp.where(jj < CAP, first + jj, -1))
    for k in range(3):
        tail = choose(jnp.where(jj >= CAP, first + 2 * k + jj - CAP, -1))
        right = [tokens_ref[:, i * part : (i + 1) * part] for i in (k, 3)]
        left, right = jnp.concatenate([head, tail], 1), jnp.concatenate(right, 0)
        rows = jnp.dot(left, right, preferred_element_type=F32).astype(BF16)
        out_ref[:, :, begin + k * part : begin + (k + 1) * part] = rows.reshape(dests, 8, part)


def pack_tokens_kernel(experts, place_ref, a_meta, b_meta, a_ref, b_ref, out_ref):
    dests = out_ref.shape[0]
    width = a_ref.shape[1]
    half, head = width // 2, 3 * width // 4
    slot = experts * CAP + iota((8, 1), 0)
    odd = (iota((dests, 1, 1), 0) & 1) == 1
    for source, (meta, in_ref) in enumerate(((a_meta, a_ref), (b_meta, b_ref))):
        fold_rows(place_ref, meta, in_ref, out_ref, experts, source * head)
        key0, key1 = slot_keys(meta[...], experts)
        left = pick((slot == key0) | (slot == key1))
        rows = jnp.dot(left, in_ref[...], preferred_element_type=F32)[None]
        first = 2 * head + source * half
        out_ref[:, :, first : first + half] = jnp.where(odd, rows[..., half:], rows[..., :half]).astype(BF16)


def pack_tokens(place, metas, tokens, experts):
    return pl.pallas_call(
        functools.partial(pack_tokens_kernel, experts),
        in_specs=[pl.BlockSpec(memory_space=pltpu.SMEM)] + [pl.BlockSpec(memory_space=pltpu.VMEM)] * 4,
        out_shape=jax.ShapeDtypeStruct((experts // 2, 8, 10 * tokens[0].shape[1] // 4), BF16),
        compiler_params=pltpu.CompilerParams(vmem_limit_bytes=VMEM_LIMIT),
        name="pack_tokens",
    )(place, *metas, *tokens)


def pack_scaled_kernel(experts, place_ref, near_ref, far_ref, out_ref):
    block, part = 2 * out_ref.shape[0], out_ref.shape[-1]
    extras = []
    tok = 128
    planes = 4
    span = planes * CAP
    first = pl.program_id(0) * block

    for source, raw in enumerate((near_ref, far_ref)):
        facts = []
        for p in range(planes):
            meta = raw[p, tok : tok + 16, 0:tok].astype(F32)
            gate0 = (meta[2:3] + meta[3:4]) + meta[4:5]
            gate1 = (meta[5:6] + meta[6:7]) + meta[7:8]
            facts.append((*slot_keys(meta[0:8], experts), gate0, gate1))
        right = jnp.concatenate([raw[p, 0:tok, :] for p in range(planes)], 0)

        def rows_of(slot, plane):
            lefts = []
            gate = jnp.zeros(slot.shape, F32)
            for p, (key0, key1, gate0, gate1) in enumerate(facts):
                mine = jnp.where(plane == p, slot, -1)
                hit0, hit1 = mine == key0, mine == key1
                both = jnp.where(hit0, gate0, 0.0) + jnp.where(hit1, gate1, 0.0)
                gate = gate + jnp.sum(both, 1, keepdims=True)
                lefts.append(pick(hit0 | hit1))
            rows = jnp.dot(jnp.concatenate(lefts, 1), right, preferred_element_type=F32)
            return (gate * rows).astype(BF16)

        row = iota((block * span, 1), 0)
        dest = floordiv(row, span)
        j = row - dest * span
        plane = floordiv(j, CAP)
        slot = expert_of(first + dest, place_ref[3]) * CAP + j - plane * CAP
        main = rows_of(slot, plane).reshape(block, span, part)
        out_ref[:, :, source * span : (source + 1) * span] = main.reshape(block // 2, 2, span, part)
        j = iota((span, 1), 0)
        plane = floordiv(j, CAP)
        extras.append(rows_of(experts * CAP + j - plane * CAP, plane))
    half = span // 2
    for core in range(2):
        extra = jnp.concatenate([e[core * half : (core + 1) * half] for e in extras], 0)
        out_ref[:, core, 2 * span :] = jnp.broadcast_to(extra[None], (block // 2, span, part))


def pack_scaled(place, near, far, experts):
    part = near.shape[-1]
    dests = experts // 2
    block = 8
    span = 4 * CAP
    return pl.pallas_call(
        functools.partial(pack_scaled_kernel, experts),
        grid_spec=pltpu.PrefetchScalarGridSpec(
            num_scalar_prefetch=1,
            grid=(dests // block,),
            in_specs=[pl.BlockSpec(near.shape, lambda g, s: (0, 0, 0))] * 2,
            out_specs=pl.BlockSpec((block // 2, 2, 3 * span, part), lambda g, s: (g, 0, 0, 0)),
        ),
        out_shape=jax.ShapeDtypeStruct((dests // 2, 2, 3 * span, part), BF16),
        compiler_params=pltpu.CompilerParams(vmem_limit_bytes=VMEM_LIMIT),
        name="pack_scaled",
    )(place, near, far)


def silu(v):
    return v / (1.0 + jnp.exp(-v))


def compact(senders):
    r, c = iota((senders * CAP, senders * 8), 0), iota((senders * CAP, senders * 8), 1)
    src = floordiv(r, CAP)
    s = r - src * CAP
    return src, s, c, pick(c == src * 8 + s)


def hidden_main_kernel(x_ref, w_ref, out_ref, rows_ref):
    senders = x_ref.shape[0]
    width = w_ref.shape[0]
    part = width // 4
    head = 3 * part

    @pl.when(pl.program_id(0) == 0)
    def _():
        src, s, c, choose = compact(senders)
        for source in range(2):
            x = x_ref[:, :, source * head : (source + 1) * head].reshape(senders * 8, head)
            first = source * senders * CAP
            into = slice(first, first + senders * CAP)
            rows_ref[into, 0:head] = jnp.dot(choose, x, preferred_element_type=F32).astype(BF16)
            tail = jnp.zeros((senders * CAP, part), F32)
            for k in range(3):
                mask = (c == src * 8 + CAP + s - 2 * k) & (s >= 2 * k) & (s < 2 * k + 2)
                tail = tail + jnp.dot(
                    pick(mask), x[:, k * part : (k + 1) * part], preferred_element_type=F32
                )
            rows_ref[into, head:] = tail.astype(BF16)

    v = jnp.dot(rows_ref[...], w_ref[...], preferred_element_type=F32)
    out_ref[...] = silu(v).astype(BF16)


def hidden_main(x, weight):
    senders = x.shape[0]
    width, hid = weight.shape
    count = 2 * senders * CAP
    block = 256
    return pl.pallas_call(
        hidden_main_kernel,
        grid=(hid // block,),
        in_specs=[
            pl.BlockSpec((senders, 8, 6 * width // 4), lambda n: (0, 0, 0)),
            pl.BlockSpec((width, block), lambda n: (0, n)),
        ],
        out_specs=pl.BlockSpec((count, block), lambda n: (0, n)),
        out_shape=jax.ShapeDtypeStruct((count, hid), BF16),
        scratch_shapes=[pltpu.VMEM((count, width), BF16)],
        compiler_params=pltpu.CompilerParams(vmem_limit_bytes=VMEM_LIMIT),
        name="hidden_main",
    )(x, weight)


def hidden_extra_kernel(place_ref, near_ref, far_ref, w_ref, out_ref, rows_ref):
    senders, _, width = near_ref.shape
    half = width // 2
    count = senders * CAP
    is_hot = place_ref[0] > 0

    @pl.when(is_hot & (pl.program_id(0) == 0))
    def _():
        choose = compact(senders)[-1]

        def put(x_ref, first):
            for source in range(2):
                x = x_ref[:, :, source * half : (source + 1) * half].reshape(senders * 8, half)
                rows = jnp.dot(choose, x, preferred_element_type=F32).astype(BF16)
                rows_ref[source * count : (source + 1) * count, first : first + half] = rows

        for core in range(2):

            @pl.when(place_ref[2] == core)
            def _():
                put(near_ref, core * half)
                put(far_ref, (1 - core) * half)

    @pl.when(is_hot)
    def _():
        v = jnp.dot(rows_ref[...], w_ref[...], preferred_element_type=F32)
        out_ref[...] = silu(v).astype(BF16)

    @pl.when(jnp.logical_not(is_hot))
    def _():
        out_ref[...] = jnp.zeros_like(out_ref)


def hidden_extra(place, near, far, weight):
    senders = near.shape[0]
    width, hid = weight.shape
    count = 2 * senders * CAP
    block = 256
    x_spec = pl.BlockSpec(near.shape, lambda n, s: (0, 0, 0))
    return pl.pallas_call(
        hidden_extra_kernel,
        grid_spec=pltpu.PrefetchScalarGridSpec(
            num_scalar_prefetch=1,
            grid=(hid // block,),
            in_specs=[x_spec, x_spec, pl.BlockSpec((width, block), lambda n, s: (0, n))],
            out_specs=pl.BlockSpec((count, block), lambda n, s: (0, n)),
            scratch_shapes=[pltpu.VMEM((count, width), BF16)],
        ),
        out_shape=jax.ShapeDtypeStruct((count, hid), BF16),
        compiler_params=pltpu.CompilerParams(vmem_limit_bytes=VMEM_LIMIT),
        name="hidden_extra",
    )(place, near, far, weight)


GROUP = 16


def by_plane(planes):
    n = GROUP * CAP
    rows = planes * 2 * n
    o, i = iota((rows, rows), 0), iota((rows, rows), 1)
    pair = floordiv(o, n)
    rest = o - pair * n
    plane, source = pair >> 1, pair & 1
    sender = floordiv(rest, CAP)
    return pick(i == ((sender * 2 + source) * planes + plane) * CAP + rest - sender * CAP)


def grad_kernel(place_ref, near_ref, far_ref, x0, x1, x2, x3, s_ref, here_ref, there_ref, out_ref, acc_ref):
    planes, _, _, hid = near_ref.shape
    part = s_ref.shape[-1]
    g = pl.program_id(0)

    def ordered(s, count):
        s = s.reshape(count * 2 * GROUP * CAP, part)
        return jnp.dot(by_plane(count), s, preferred_element_type=F32).astype(BF16)

    def total(hs, s):
        h = jnp.concatenate(hs, 0)
        return lax.dot_general(h, s, (((0,), (0,)), ((), ())), preferred_element_type=F32)

    sender = floordiv(iota((near_ref.shape[2], 1), 0), CAP)
    is_z = place_ref[3]
    even, odd = pick((sender & 1) == 0), pick((sender & 1) == 1)
    odd_z = [pick(((sender & 1) == 1) & (is_z == z)) for z in range(2)]

    def main():
        hs = []
        for d in range(planes):
            plane = place_ref[1] + planes - d
            other = lax.rem(plane + 1 - 2 * is_z, planes)
            plane = lax.rem(plane, planes)
            hs += [near_ref[plane, 0], far_ref[plane, 0] * even + far_ref[other, 0] * odd]
        return total(hs, ordered(s_ref[...], planes))

    @pl.when(g == 0)
    def _():
        acc_ref[...] = main()

    @pl.when(g > 0)
    def _():
        acc_ref[...] += main()

    for core in range(2):

        @pl.when((place_ref[0] > 0) & (place_ref[2] == core))
        def _():
            here, there = ordered(here_ref[...], planes // 2), ordered(there_ref[...], planes // 2)
            s = jnp.concatenate([there, here] if core else [here, there], 0)
            xs = (x0, x1, x2, x3)
            hs = []
            for d in range(planes):
                other = xs[d - 1][1] * odd_z[0] + xs[(d + 1) % planes][1] * odd_z[1]
                hs += [xs[d][0], xs[d][1] * even + other]
            acc_ref[...] += total(hs, s)

    @pl.when(g == pl.num_programs(0) - 1)
    def _():
        out_ref[...] = acc_ref[...].astype(out_ref.dtype)


def grad_of(place, hidden, extras, s, here, there):
    planes, _, hid = hidden.shape
    senders, span, part = here.shape
    n = GROUP * CAP
    hidden = hidden.reshape(planes, 2, -1, hid)
    h_specs = [pl.BlockSpec((planes, 1, n, hid), lambda g, s, i=i: (0, i, g, 0)) for i in range(2)]
    x_spec = pl.BlockSpec((2, n, hid), lambda g, s: (0, g, 0))
    half = pl.BlockSpec((GROUP, span, part), lambda g, s: (g, 0, 0))
    return pl.pallas_call(
        grad_kernel,
        grid_spec=pltpu.PrefetchScalarGridSpec(
            num_scalar_prefetch=1,
            grid=(senders // GROUP,),
            in_specs=h_specs
            + [x_spec] * 4
            + [pl.BlockSpec((GROUP, 2 * span, part), lambda g, s: (g, 0, 0)), half, half],
            out_specs=pl.BlockSpec((hid, part), lambda g, s: (0, 0)),
            scratch_shapes=[pltpu.VMEM((hid, part), F32)],
        ),
        out_shape=jax.ShapeDtypeStruct((hid, part), BF16),
        compiler_params=pltpu.CompilerParams(vmem_limit_bytes=VMEM_LIMIT),
        name="grad_of",
    )(place, hidden, hidden, *[x.reshape(2, -1, hid) for x in extras], s, here, there)


def join_kernel(in_ref, out_ref):
    out_ref[...] = in_ref[...].astype(F32)


def join(parts):
    planes, rows, part = parts.shape
    return pl.pallas_call(
        join_kernel,
        grid=(planes,),
        in_specs=[pl.BlockSpec((1, rows, part), lambda n: (n, 0, 0))],
        out_specs=pl.BlockSpec((1, rows, part), lambda n: (0, 0, n)),
        out_shape=jax.ShapeDtypeStruct((1, rows, planes * part), F32),
        compiler_params=pltpu.CompilerParams(vmem_limit_bytes=VMEM_LIMIT),
        name="join",
    )(parts)


def bf16_parts(x):
    high = lax.reduce_precision(x, 8, 7)
    mid = lax.reduce_precision(x - high, 8, 7)
    return [high, mid, x - high - mid]


def z_neighbours(experts, planes):
    pairs = []
    for e in range(experts):
        step = 0 if e & 1 == 0 else (1 if (e >> 3) & 1 else -1)
        pairs += [(e * planes + p, (e ^ 8) * planes + (p + step) % planes) for p in range(planes)]
    return pairs


def local(tokens, cotangent, routes, gates, gate_weight):
    experts = lax.axis_size("expert")
    planes = lax.axis_size("dp")
    me = lax.axis_index("expert")
    dp = lax.axis_index("dp")
    core = me & 1
    other_z = [(i, i ^ 8) for i in range(experts)]
    other_core = [(i, i ^ 1) for i in range(experts)]
    same_z = [[i for i in range(experts) if (i >> 3) & 1 == z] for z in range(2)]

    route_rows = routes.T.astype(F32)
    gate_rows = gates.T
    meta = jnp.concatenate(
        [route_rows, jnp.stack(bf16_parts(gate_rows[0])), jnp.stack(bf16_parts(gate_rows[1]))], 0
    )
    named = (routes.reshape(-1)[:, None] == jnp.arange(experts, dtype=jnp.int32)[None, :]).astype(F32)
    hot_expert = jnp.argmax(jnp.sum(named, 0)).astype(jnp.int32)
    hot = (hot_expert == me).astype(jnp.int32)
    place = jnp.stack([hot, dp, core, (me >> 3) & 1]).astype(jnp.int32)

    def dispatch(x):
        return lax.all_to_all(x, "expert", 0, 0, tiled=True, axis_index_groups=same_z)

    weight = gate_weight[0]

    either_z = z_neighbours(experts, planes)
    far_tokens = lax.ppermute(tokens, ("expert", "dp"), either_z)
    far_meta = lax.ppermute(meta, ("expert", "dp"), either_z)
    blocks = split_raw(place, cotangent, meta)
    far_tokens, far_meta, blocks = lax.optimization_barrier((far_tokens, far_meta, blocks))
    sent = pack_tokens(place, (meta, far_meta), (tokens, far_tokens), experts)
    arrived = dispatch(sent)

    raw = [blocks[0]]
    for d in range(1, planes):
        raw.append(lax.ppermute(blocks[d], "dp", [(i, (i + d) % planes) for i in range(planes)]))
    raw = jnp.stack(raw)
    far_raw = lax.ppermute(raw, "expert", other_z)
    scaled = pack_scaled(place, raw, far_raw, experts)
    arrived, scaled = lax.optimization_barrier((arrived, scaled))

    span = scaled.shape[-2] // 3
    scaled = dispatch(scaled.reshape(experts // 2, 3 * span, scaled.shape[-1]))

    hidden = hidden_main(arrived, weight)
    arrived, _ = lax.optimization_barrier((arrived, hidden))
    hidden = lax.all_gather(hidden, "dp")
    extra = arrived[:, :, 6 * arrived.shape[-1] // 10 :]
    far_extra = lax.ppermute(extra, "expert", other_core)
    own_extra = hidden_extra(place, extra, far_extra, weight)

    def share(z, c):
        def permutes(x):
            def shift(y, d):
                pairs = [
                    (e * planes + i, e * planes + (i + d) % planes)
                    for e in range(experts)
                    if (e >> 3) & 1 == z and e & 1 == c
                    for i in range(planes)
                ]
                return lax.ppermute(y, ("expert", "dp"), pairs)

            half = x.shape[0] // 2
            before, after = shift(x, 1), shift(x, -1)
            opposite = jnp.concatenate([shift(before[:half], 1), shift(after[half:], -1)], 0)
            return before, opposite, after

        return permutes

    table = [share(z, c) for z in range(2) for c in range(2)]
    extras = lax.switch(((hot_expert >> 3) & 1) * 2 + (hot_expert & 1), table, own_extra)

    scaled, own_extra, extras = lax.optimization_barrier((scaled, own_extra, extras))
    near_scaled = scaled[:, 2 * span :]
    far_scaled = lax.ppermute(near_scaled, "expert", other_core)
    extras = (own_extra, *extras)
    grad = grad_of(place, hidden, extras, scaled, near_scaled, far_scaled)
    hid = grad.shape[0] // planes
    grad = lax.all_to_all(grad.reshape(planes, hid, -1), "dp", 0, 0, tiled=True)
    return join(grad)


def solution(mesh):
    placed = (
        P(("expert", "dp"), None),
        P(("expert", "dp"), None),
        P(("expert", "dp"), None),
        P(("expert", "dp"), None),
        P("expert", None, None),
    )
    return jax.shard_map(
        local, mesh=mesh, in_specs=placed, out_specs=P("expert", "dp", None), check_vma=False
    )
```

```python
import functools

import jax
import jax.numpy as jnp
from jax import lax
from jax.experimental import pallas as pl
from jax.experimental.pallas import tpu as pltpu
from jax.sharding import PartitionSpec as P

CAP = 6
F32 = jnp.float32
BF16 = jnp.bfloat16
VMEM_LIMIT = 56 * 1024 * 1024


def iota(shape, dim):
    return lax.broadcasted_iota(jnp.int32, shape, dim)


def floordiv(a, n):
    return jnp.floor((a.astype(F32) + 0.5) * (1.0 / n)).astype(jnp.int32)


def slot_ranks(route):
    tok = route.shape[1]
    column = route.T
    r0, r1 = route[0:1], route[1:2]
    c0, c1 = column[:, 0:1], column[:, 1:2]
    before = iota((tok, tok), 0) < iota((tok, tok), 1)

    def count(mask):
        return jnp.sum(jnp.where(mask, 1.0, 0.0), 0, keepdims=True)

    return count((c0 == r0) & before), count(c0 == r1) + count((c1 == r1) & before)


def slot_key(r, rank, experts):
    return jnp.where(rank < CAP, r * CAP + rank, experts * CAP + rank - CAP).astype(jnp.int32)


def slot_keys(route, experts):
    rank0, rank1 = slot_ranks(route)
    return slot_key(route[0:1], rank0, experts), slot_key(route[1:2], rank1, experts)


def split_raw_kernel(place_ref, q0_ref, q1_ref, q2_ref, q3_ref, meta_ref, *out_refs):
    tok, part = q0_ref.shape
    ranks = jnp.concatenate([*slot_ranks(meta_ref[...]), jnp.zeros((6, tok), F32)], 0)
    note = jnp.concatenate([meta_ref[...], ranks], 0).astype(BF16)
    note = jnp.concatenate([note, jnp.zeros((16, part - tok), BF16)], 1)
    for in_ref, out_ref in zip((q0_ref, q1_ref, q2_ref, q3_ref), out_refs):
        out_ref[0:tok, :] = in_ref[...]
        out_ref[tok:, :] = note


def split_raw(place, cotangent, meta):
    tok, width = cotangent.shape
    part = width // 4
    quarter = [pl.BlockSpec((tok, part), lambda i, s, d=d: (0, lax.rem(s[1] + d, 4))) for d in range(4)]
    return pl.pallas_call(
        split_raw_kernel,
        grid_spec=pltpu.PrefetchScalarGridSpec(
            num_scalar_prefetch=1,
            grid=(1,),
            in_specs=quarter + [pl.BlockSpec(meta.shape, lambda i, s: (0, 0))],
            out_specs=[pl.BlockSpec((tok + 16, part), lambda i, s: (0, 0))] * 4,
        ),
        out_shape=[jax.ShapeDtypeStruct((tok + 16, part), BF16)] * 4,
        compiler_params=pltpu.CompilerParams(vmem_limit_bytes=VMEM_LIMIT),
        name="split_raw",
    )(place, cotangent, cotangent, cotangent, cotangent, meta)


def pick(mask):
    return jnp.where(mask, 1.0, 0.0).astype(BF16)


def expert_of(dest, z):
    return (dest >> 3) * 16 + z * 8 + (dest & 7)


def fold_rows(place_ref, meta_ref, tokens_ref, out_ref, experts, begin):
    dests = out_ref.shape[0]
    part = tokens_ref.shape[1] // 4
    key0, key1 = slot_keys(meta_ref[...], experts)
    row = iota((dests * 8, 1), 0)
    jj = row & 7
    first = expert_of(row >> 3, place_ref[3]) * CAP

    def choose(slot):
        return pick((slot == key0) | (slot == key1))

    head = choose(jnp.where(jj < CAP, first + jj, -1))
    for k in range(3):
        tail = choose(jnp.where(jj >= CAP, first + 2 * k + jj - CAP, -1))
        right = [tokens_ref[:, i * part : (i + 1) * part] for i in (k, 3)]
        left, right = jnp.concatenate([head, tail], 1), jnp.concatenate(right, 0)
        rows = jnp.dot(left, right, preferred_element_type=F32).astype(BF16)
        out_ref[:, :, begin + k * part : begin + (k + 1) * part] = rows.reshape(dests, 8, part)


def pack_tokens_kernel(experts, place_ref, a_meta, b_meta, a_ref, b_ref, out_ref):
    dests = out_ref.shape[0]
    width = a_ref.shape[1]
    half, head = width // 2, 3 * width // 4
    slot = experts * CAP + iota((8, 1), 0)
    odd = (iota((dests, 1, 1), 0) & 1) == 1
    for source, (meta, in_ref) in enumerate(((a_meta, a_ref), (b_meta, b_ref))):
        fold_rows(place_ref, meta, in_ref, out_ref, experts, source * head)
        key0, key1 = slot_keys(meta[...], experts)
        left = pick((slot == key0) | (slot == key1))
        rows = jnp.dot(left, in_ref[...], preferred_element_type=F32)[None]
        first = 2 * head + source * half
        out_ref[:, :, first : first + half] = jnp.where(odd, rows[..., half:], rows[..., :half]).astype(BF16)


def pack_tokens(place, metas, tokens, experts):
    return pl.pallas_call(
        functools.partial(pack_tokens_kernel, experts),
        in_specs=[pl.BlockSpec(memory_space=pltpu.SMEM)] + [pl.BlockSpec(memory_space=pltpu.VMEM)] * 4,
        out_shape=jax.ShapeDtypeStruct((experts // 2, 8, 10 * tokens[0].shape[1] // 4), BF16),
        compiler_params=pltpu.CompilerParams(vmem_limit_bytes=VMEM_LIMIT),
        name="pack_tokens",
    )(place, *metas, *tokens)


def pack_scaled_kernel(experts, place_ref, own_ref, moved_ref, far_own_ref, far_moved_ref, out_ref):
    block, part = 2 * out_ref.shape[0], out_ref.shape[-1]
    extras = []
    tok = 128
    planes = 4
    span = planes * CAP
    first = pl.program_id(0) * block

    for source, (first_ref, others_ref) in enumerate(((own_ref, moved_ref), (far_own_ref, far_moved_ref))):
        raws = [first_ref[...]] + [others_ref[p] for p in range(planes - 1)]
        facts = []
        for p in range(planes):
            meta = raws[p][tok : tok + 16, 0:tok].astype(F32)
            gate0 = (meta[2:3] + meta[3:4]) + meta[4:5]
            gate1 = (meta[5:6] + meta[6:7]) + meta[7:8]
            keys = [slot_key(meta[i : i + 1], meta[8 + i : 9 + i], experts) for i in range(2)]
            facts.append((*keys, gate0, gate1))
        right = jnp.concatenate([raw[0:tok, :] for raw in raws], 0)

        def rows_of(slot, plane):
            lefts = []
            gate = jnp.zeros(slot.shape, F32)
            for p, (key0, key1, gate0, gate1) in enumerate(facts):
                mine = jnp.where(plane == p, slot, -1)
                hit0, hit1 = mine == key0, mine == key1
                both = jnp.where(hit0, gate0, 0.0) + jnp.where(hit1, gate1, 0.0)
                gate = gate + jnp.sum(both, 1, keepdims=True)
                lefts.append(pick(hit0 | hit1))
            rows = jnp.dot(jnp.concatenate(lefts, 1), right, preferred_element_type=F32)
            return (gate * rows).astype(BF16)

        row = iota((block * span, 1), 0)
        dest = floordiv(row, span)
        j = row - dest * span
        plane = floordiv(j, CAP)
        slot = expert_of(first + dest, place_ref[3]) * CAP + j - plane * CAP
        main = rows_of(slot, plane).reshape(block, span, part)
        out_ref[:, :, source * span : (source + 1) * span] = main.reshape(block // 2, 2, span, part)
        j = iota((span, 1), 0)
        plane = floordiv(j, CAP)
        extras.append(rows_of(experts * CAP + j - plane * CAP, plane))
    half = span // 2
    for core in range(2):
        extra = jnp.concatenate([e[core * half : (core + 1) * half] for e in extras], 0)
        out_ref[:, core, 2 * span :] = jnp.broadcast_to(extra[None], (block // 2, span, part))


def pack_scaled(place, raws, experts):
    part = raws[0].shape[-1]
    dests = experts // 2
    block = 8
    span = 4 * CAP
    return pl.pallas_call(
        functools.partial(pack_scaled_kernel, experts),
        grid_spec=pltpu.PrefetchScalarGridSpec(
            num_scalar_prefetch=1,
            grid=(dests // block,),
            in_specs=[pl.BlockSpec(r.shape, lambda g, s, n=r.ndim: (0,) * n) for r in raws],
            out_specs=pl.BlockSpec((block // 2, 2, 3 * span, part), lambda g, s: (g, 0, 0, 0)),
        ),
        out_shape=jax.ShapeDtypeStruct((dests // 2, 2, 3 * span, part), BF16),
        compiler_params=pltpu.CompilerParams(vmem_limit_bytes=VMEM_LIMIT),
        name="pack_scaled",
    )(place, *raws)


def silu(v):
    return v / (1.0 + jnp.exp(-v))


def compact(senders):
    r, c = iota((senders * CAP, 1), 0), iota((senders * CAP, senders * 8), 1)
    src = floordiv(r, CAP)
    s = r - src * CAP
    return src, s, c, pick(c == src * 8 + s)


def hidden_main_kernel(x_ref, w_ref, out_ref, rows_ref):
    senders = x_ref.shape[0]
    width = w_ref.shape[0]
    part = width // 4
    head = 3 * part

    @pl.when(pl.program_id(0) == 0)
    def _():
        src, s, c, choose = compact(senders)
        for source in range(2):
            x = x_ref[:, :, source * head : (source + 1) * head].reshape(senders * 8, head)
            first = source * senders * CAP
            into = slice(first, first + senders * CAP)
            rows_ref[into, 0:head] = jnp.dot(choose, x, preferred_element_type=F32).astype(BF16)
            tail = jnp.zeros((senders * CAP, part), F32)
            for k in range(3):
                held = (s >= 2 * k) & (s < 2 * k + 2)
                mask = c == jnp.where(held, src * 8 + CAP + s - 2 * k, -1)
                tail = tail + jnp.dot(
                    pick(mask), x[:, k * part : (k + 1) * part], preferred_element_type=F32
                )
            rows_ref[into, head:] = tail.astype(BF16)

    v = jnp.dot(rows_ref[...], w_ref[...], preferred_element_type=F32)
    out_ref[...] = silu(v).astype(BF16)


def hidden_main(x, weight):
    senders = x.shape[0]
    width, hid = weight.shape
    count = 2 * senders * CAP
    block = 256
    return pl.pallas_call(
        hidden_main_kernel,
        grid=(hid // block,),
        in_specs=[
            pl.BlockSpec((senders, 8, 6 * width // 4), lambda n: (0, 0, 0)),
            pl.BlockSpec((width, block), lambda n: (0, n)),
        ],
        out_specs=pl.BlockSpec((count, block), lambda n: (0, n)),
        out_shape=jax.ShapeDtypeStruct((count, hid), BF16),
        scratch_shapes=[pltpu.VMEM((count, width), BF16)],
        compiler_params=pltpu.CompilerParams(vmem_limit_bytes=VMEM_LIMIT),
        name="hidden_main",
    )(x, weight)


def hidden_extra_kernel(place_ref, near_ref, far_ref, w_ref, out_ref, rows_ref):
    senders, _, width = near_ref.shape
    half = width // 2
    count = senders * CAP
    is_hot = place_ref[0] > 0

    @pl.when(is_hot & (pl.program_id(0) == 0))
    def _():
        choose = compact(senders)[-1]

        def put(x_ref, first):
            for source in range(2):
                x = x_ref[:, :, source * half : (source + 1) * half].reshape(senders * 8, half)
                rows = jnp.dot(choose, x, preferred_element_type=F32).astype(BF16)
                rows_ref[source * count : (source + 1) * count, first : first + half] = rows

        for core in range(2):

            @pl.when(place_ref[2] == core)
            def _():
                put(near_ref, core * half)
                put(far_ref, (1 - core) * half)

    @pl.when(is_hot)
    def _():
        v = jnp.dot(rows_ref[...], w_ref[...], preferred_element_type=F32)
        out_ref[...] = silu(v).astype(BF16)

    @pl.when(jnp.logical_not(is_hot))
    def _():
        out_ref[...] = jnp.zeros_like(out_ref)


def hidden_extra(place, near, far, weight):
    senders = near.shape[0]
    width, hid = weight.shape
    count = 2 * senders * CAP
    block = 256
    x_spec = pl.BlockSpec(near.shape, lambda n, s: (0, 0, 0))
    return pl.pallas_call(
        hidden_extra_kernel,
        grid_spec=pltpu.PrefetchScalarGridSpec(
            num_scalar_prefetch=1,
            grid=(hid // block,),
            in_specs=[x_spec, x_spec, pl.BlockSpec((width, block), lambda n, s: (0, n))],
            out_specs=pl.BlockSpec((count, block), lambda n, s: (0, n)),
            scratch_shapes=[pltpu.VMEM((count, width), BF16)],
        ),
        out_shape=jax.ShapeDtypeStruct((count, hid), BF16),
        compiler_params=pltpu.CompilerParams(vmem_limit_bytes=VMEM_LIMIT),
        name="hidden_extra",
    )(place, near, far, weight)


GROUP = 16


def by_plane(planes):
    n = GROUP * CAP
    rows = planes * 2 * n
    o = iota((rows, 1), 0)
    pair = floordiv(o, n)
    rest = o - pair * n
    plane, source = pair >> 1, pair & 1
    sender = floordiv(rest, CAP)
    origin = ((sender * 2 + source) * planes + plane) * CAP + rest - sender * CAP
    return pick(iota((rows, rows), 1) == origin)


def grad_kernel(place_ref, near_ref, far_ref, x0, x1, x2, x3, s_ref, here_ref, there_ref, out_ref, acc_ref):
    planes, _, _, hid = near_ref.shape
    part = s_ref.shape[-1]
    g = pl.program_id(0)

    def ordered(s, count):
        s = s.reshape(count * 2 * GROUP * CAP, part)
        return jnp.dot(by_plane(count), s, preferred_element_type=F32).astype(BF16)

    def total(hs, s):
        h = jnp.concatenate(hs, 0)
        return lax.dot_general(h, s, (((0,), (0,)), ((), ())), preferred_element_type=F32)

    sender = floordiv(iota((near_ref.shape[2], 1), 0), CAP)
    is_z = place_ref[3]
    even, odd = pick((sender & 1) == 0), pick((sender & 1) == 1)
    odd_z = [pick(((sender & 1) == 1) & (is_z == z)) for z in range(2)]

    def main():
        hs = []
        for d in range(planes):
            plane = place_ref[1] + planes - d
            other = lax.rem(plane + 1 - 2 * is_z, planes)
            plane = lax.rem(plane, planes)
            hs += [near_ref[plane, 0], far_ref[plane, 0] * even + far_ref[other, 0] * odd]
        return total(hs, ordered(s_ref[...], planes))

    @pl.when(g == 0)
    def _():
        acc_ref[...] = main()

    @pl.when(g > 0)
    def _():
        acc_ref[...] += main()

    for core in range(2):

        @pl.when((place_ref[0] > 0) & (place_ref[2] == core))
        def _():
            here, there = ordered(here_ref[...], planes // 2), ordered(there_ref[...], planes // 2)
            s = jnp.concatenate([there, here] if core else [here, there], 0)
            xs = (x0, x1, x2, x3)
            hs = []
            for d in range(planes):
                other = xs[d - 1][1] * odd_z[0] + xs[(d + 1) % planes][1] * odd_z[1]
                hs += [xs[d][0], xs[d][1] * even + other]
            acc_ref[...] += total(hs, s)

    @pl.when(g == pl.num_programs(0) - 1)
    def _():
        out_ref[...] = acc_ref[...].astype(out_ref.dtype)


def grad_of(place, hidden, extras, s, here, there):
    planes, _, hid = hidden.shape
    senders, span, part = here.shape
    n = GROUP * CAP
    hidden = hidden.reshape(planes, 2, -1, hid)
    h_specs = [pl.BlockSpec((planes, 1, n, hid), lambda g, s, i=i: (0, i, g, 0)) for i in range(2)]
    x_spec = pl.BlockSpec((2, n, hid), lambda g, s: (0, g, 0))
    half = pl.BlockSpec((GROUP, span, part), lambda g, s: (g, 0, 0))
    return pl.pallas_call(
        grad_kernel,
        grid_spec=pltpu.PrefetchScalarGridSpec(
            num_scalar_prefetch=1,
            grid=(senders // GROUP,),
            in_specs=h_specs
            + [x_spec] * 4
            + [pl.BlockSpec((GROUP, 2 * span, part), lambda g, s: (g, 0, 0)), half, half],
            out_specs=pl.BlockSpec((hid, part), lambda g, s: (0, 0)),
            scratch_shapes=[pltpu.VMEM((hid, part), F32)],
        ),
        out_shape=jax.ShapeDtypeStruct((hid, part), BF16),
        compiler_params=pltpu.CompilerParams(vmem_limit_bytes=VMEM_LIMIT),
        name="grad_of",
    )(place, hidden, hidden, *[x.reshape(2, -1, hid) for x in extras], s, here, there)


def join_kernel(in_ref, out_ref):
    out_ref[...] = in_ref[...].astype(F32)


def join(parts):
    planes, rows, part = parts.shape
    return pl.pallas_call(
        join_kernel,
        grid=(planes,),
        in_specs=[pl.BlockSpec((1, rows, part), lambda n: (n, 0, 0))],
        out_specs=pl.BlockSpec((1, rows, part), lambda n: (0, 0, n)),
        out_shape=jax.ShapeDtypeStruct((1, rows, planes * part), F32),
        compiler_params=pltpu.CompilerParams(vmem_limit_bytes=VMEM_LIMIT),
        name="join",
    )(parts)


def bf16_parts(x):
    high = lax.reduce_precision(x, 8, 7)
    mid = lax.reduce_precision(x - high, 8, 7)
    return [high, mid, x - high - mid]


def z_neighbours(experts, planes):
    pairs = []
    for e in range(experts):
        step = 0 if e & 1 == 0 else (1 if (e >> 3) & 1 else -1)
        pairs += [(e * planes + p, (e ^ 8) * planes + (p + step) % planes) for p in range(planes)]
    return pairs


def local(tokens, cotangent, routes, gates, gate_weight):
    experts = lax.axis_size("expert")
    planes = lax.axis_size("dp")
    me = lax.axis_index("expert")
    dp = lax.axis_index("dp")
    core = me & 1
    other_z = [(i, i ^ 8) for i in range(experts)]
    other_core = [(i, i ^ 1) for i in range(experts)]
    same_z = [[i for i in range(experts) if (i >> 3) & 1 == z] for z in range(2)]

    route_rows = routes.T.astype(F32)
    gate_rows = gates.T
    meta = jnp.concatenate(
        [route_rows, jnp.stack(bf16_parts(gate_rows[0])), jnp.stack(bf16_parts(gate_rows[1]))], 0
    )
    named = (routes.reshape(-1)[:, None] == jnp.arange(experts, dtype=jnp.int32)[None, :]).astype(F32)
    hot_expert = jnp.argmax(jnp.sum(named, 0)).astype(jnp.int32)
    hot = (hot_expert == me).astype(jnp.int32)
    place = jnp.stack([hot, dp, core, (me >> 3) & 1]).astype(jnp.int32)

    def dispatch(x):
        return lax.all_to_all(x, "expert", 0, 0, tiled=True, axis_index_groups=same_z)

    weight = gate_weight[0]

    either_z = z_neighbours(experts, planes)
    far_tokens = lax.ppermute(tokens, ("expert", "dp"), either_z)
    far_meta = lax.ppermute(meta, ("expert", "dp"), either_z)
    blocks = split_raw(place, cotangent, meta)
    far_tokens, far_meta, blocks = lax.optimization_barrier((far_tokens, far_meta, blocks))
    sent = pack_tokens(place, (meta, far_meta), (tokens, far_tokens), experts)
    arrived = dispatch(sent)

    raw = [blocks[0]]
    for d in range(1, planes):
        raw.append(lax.ppermute(blocks[d], "dp", [(i, (i + d) % planes) for i in range(planes)]))
    far_own = lax.ppermute(blocks[0], "expert", other_z)
    far_own, raw = lax.optimization_barrier((far_own, raw))
    moved = jnp.stack(raw[1:])
    far_moved = lax.ppermute(moved, "expert", other_z)
    scaled = pack_scaled(place, (blocks[0], moved, far_own, far_moved), experts)
    arrived, scaled = lax.optimization_barrier((arrived, scaled))

    span = scaled.shape[-2] // 3
    scaled = dispatch(scaled.reshape(experts // 2, 3 * span, scaled.shape[-1]))

    hidden = hidden_main(arrived, weight)
    arrived, _ = lax.optimization_barrier((arrived, hidden))
    hidden = lax.all_gather(hidden, "dp")
    extra = arrived[:, :, 6 * arrived.shape[-1] // 10 :]
    far_extra = lax.ppermute(extra, "expert", other_core)
    own_extra = hidden_extra(place, extra, far_extra, weight)

    def share(z, c):
        def permutes(x):
            def shift(y, d):
                pairs = [
                    (e * planes + i, e * planes + (i + d) % planes)
                    for e in range(experts)
                    if (e >> 3) & 1 == z and e & 1 == c
                    for i in range(planes)
                ]
                return lax.ppermute(y, ("expert", "dp"), pairs)

            half = x.shape[0] // 2
            before, after = shift(x, 1), shift(x, -1)
            opposite = jnp.concatenate([shift(before[:half], 1), shift(after[half:], -1)], 0)
            return before, opposite, after

        return permutes

    table = [share(z, c) for z in range(2) for c in range(2)]
    extras = lax.switch(((hot_expert >> 3) & 1) * 2 + (hot_expert & 1), table, own_extra)

    scaled, own_extra, extras = lax.optimization_barrier((scaled, own_extra, extras))
    near_scaled = scaled[:, 2 * span :]
    far_scaled = lax.ppermute(near_scaled, "expert", other_core)
    extras = (own_extra, *extras)
    grad = grad_of(place, hidden, extras, scaled, near_scaled, far_scaled)
    hid = grad.shape[0] // planes
    grad = lax.all_to_all(grad.reshape(planes, hid, -1), "dp", 0, 0, tiled=True)
    return join(grad)


def solution(mesh):
    placed = (
        P(("expert", "dp"), None),
        P(("expert", "dp"), None),
        P(("expert", "dp"), None),
        P(("expert", "dp"), None),
        P("expert", None, None),
    )
    return jax.shard_map(
        local, mesh=mesh, in_specs=placed, out_specs=P("expert", "dp", None), check_vma=False
    )
```

```python
import functools

import jax
import jax.numpy as jnp
from jax import lax
from jax.experimental import pallas as pl
from jax.experimental.pallas import tpu as pltpu
from jax.sharding import PartitionSpec as P

CAP = 6
F32 = jnp.float32
BF16 = jnp.bfloat16
VMEM_LIMIT = 56 * 1024 * 1024


def iota(shape, dim):
    return lax.broadcasted_iota(jnp.int32, shape, dim)


def floordiv(a, n):
    return jnp.floor((a.astype(F32) + 0.5) * (1.0 / n)).astype(jnp.int32)


def slot_ranks(route):
    tok = route.shape[1]
    column = route.T
    r0, r1 = route[0:1], route[1:2]
    c0, c1 = column[:, 0:1], column[:, 1:2]
    before = iota((tok, tok), 0) < iota((tok, tok), 1)

    def count(mask):
        return jnp.sum(jnp.where(mask, 1.0, 0.0), 0, keepdims=True)

    return count((c0 == r0) & before), count(c0 == r1) + count((c1 == r1) & before)


def slot_key(r, rank, experts):
    return jnp.where(rank < CAP, r * CAP + rank, experts * CAP + rank - CAP).astype(jnp.int32)


def slot_keys(route, experts):
    rank0, rank1 = slot_ranks(route)
    return slot_key(route[0:1], rank0, experts), slot_key(route[1:2], rank1, experts)


def split_raw_kernel(place_ref, q0_ref, q1_ref, q2_ref, q3_ref, meta_ref, *out_refs):
    tok, part = q0_ref.shape
    ranks = jnp.concatenate([*slot_ranks(meta_ref[...]), jnp.zeros((6, tok), F32)], 0)
    note = jnp.concatenate([meta_ref[...], ranks], 0).astype(BF16)
    note = jnp.concatenate([note, jnp.zeros((16, part - tok), BF16)], 1)
    for in_ref, out_ref in zip((q0_ref, q1_ref, q2_ref, q3_ref), out_refs):
        out_ref[0:tok, :] = in_ref[...]
        out_ref[tok:, :] = note


def split_raw(place, cotangent, meta):
    tok, width = cotangent.shape
    part = width // 4
    quarter = [pl.BlockSpec((tok, part), lambda i, s, d=d: (0, lax.rem(s[1] + d, 4))) for d in range(4)]
    return pl.pallas_call(
        split_raw_kernel,
        grid_spec=pltpu.PrefetchScalarGridSpec(
            num_scalar_prefetch=1,
            grid=(1,),
            in_specs=quarter + [pl.BlockSpec(meta.shape, lambda i, s: (0, 0))],
            out_specs=[pl.BlockSpec((tok + 16, part), lambda i, s: (0, 0))] * 4,
        ),
        out_shape=[jax.ShapeDtypeStruct((tok + 16, part), BF16)] * 4,
        compiler_params=pltpu.CompilerParams(vmem_limit_bytes=VMEM_LIMIT),
        name="split_raw",
    )(place, cotangent, cotangent, cotangent, cotangent, meta)


def pick(mask):
    return jnp.where(mask, 1.0, 0.0).astype(BF16)


def expert_of(dest, z):
    return (dest >> 3) * 16 + z * 8 + (dest & 7)


def fold_rows(place_ref, meta_ref, tokens_ref, out_ref, experts, begin):
    dests = out_ref.shape[0]
    part = tokens_ref.shape[1] // 4
    key0, key1 = slot_keys(meta_ref[...], experts)
    row = iota((dests * 8, 1), 0)
    jj = row & 7
    first = expert_of(row >> 3, place_ref[3]) * CAP

    def choose(slot):
        return pick((slot == key0) | (slot == key1))

    head = choose(jnp.where(jj < CAP, first + jj, -1))
    for k in range(3):
        tail = choose(jnp.where(jj >= CAP, first + 2 * k + jj - CAP, -1))
        right = [tokens_ref[:, i * part : (i + 1) * part] for i in (k, 3)]
        left, right = jnp.concatenate([head, tail], 1), jnp.concatenate(right, 0)
        rows = jnp.dot(left, right, preferred_element_type=F32).astype(BF16)
        out_ref[:, :, begin + k * part : begin + (k + 1) * part] = rows.reshape(dests, 8, part)


def pack_tokens_kernel(experts, place_ref, a_meta, b_meta, a_ref, b_ref, out_ref):
    dests = out_ref.shape[0]
    width = a_ref.shape[1]
    half, head = width // 2, 3 * width // 4
    slot = experts * CAP + iota((8, 1), 0)
    odd = (iota((dests, 1, 1), 0) & 1) == 1
    for source, (meta, in_ref) in enumerate(((a_meta, a_ref), (b_meta, b_ref))):
        fold_rows(place_ref, meta, in_ref, out_ref, experts, source * head)
        key0, key1 = slot_keys(meta[...], experts)
        left = pick((slot == key0) | (slot == key1))
        rows = jnp.dot(left, in_ref[...], preferred_element_type=F32)[None]
        first = 2 * head + source * half
        out_ref[:, :, first : first + half] = jnp.where(odd, rows[..., half:], rows[..., :half]).astype(BF16)


def pack_tokens(place, metas, tokens, experts):
    return pl.pallas_call(
        functools.partial(pack_tokens_kernel, experts),
        in_specs=[pl.BlockSpec(memory_space=pltpu.SMEM)] + [pl.BlockSpec(memory_space=pltpu.VMEM)] * 4,
        out_shape=jax.ShapeDtypeStruct((experts // 2, 8, 10 * tokens[0].shape[1] // 4), BF16),
        compiler_params=pltpu.CompilerParams(vmem_limit_bytes=VMEM_LIMIT),
        name="pack_tokens",
    )(place, *metas, *tokens)


def pack_scaled_kernel(experts, place_ref, own_ref, moved_ref, far_own_ref, far_moved_ref, out_ref):
    block, _, part = out_ref.shape
    extras = []
    tok = 128
    planes = 4
    span = planes * CAP
    first = pl.program_id(0) * block

    for source, (first_ref, others_ref) in enumerate(((own_ref, moved_ref), (far_own_ref, far_moved_ref))):
        raws = [first_ref[...]] + [others_ref[p] for p in range(planes - 1)]
        facts = []
        for p in range(planes):
            meta = raws[p][tok : tok + 16, 0:tok].astype(F32)
            gate0 = (meta[2:3] + meta[3:4]) + meta[4:5]
            gate1 = (meta[5:6] + meta[6:7]) + meta[7:8]
            keys = [slot_key(meta[i : i + 1], meta[8 + i : 9 + i], experts) for i in range(2)]
            facts.append((*keys, gate0, gate1))
        right = jnp.concatenate([raw[0:tok, :] for raw in raws], 0)

        def rows_of(slot, plane):
            lefts = []
            gate = jnp.zeros(slot.shape, F32)
            for p, (key0, key1, gate0, gate1) in enumerate(facts):
                mine = jnp.where(plane == p, slot, -1)
                hit0, hit1 = mine == key0, mine == key1
                both = jnp.where(hit0, gate0, 0.0) + jnp.where(hit1, gate1, 0.0)
                gate = gate + jnp.sum(both, 1, keepdims=True)
                lefts.append(pick(hit0 | hit1))
            rows = jnp.dot(jnp.concatenate(lefts, 1), right, preferred_element_type=F32)
            return (gate * rows).astype(BF16)

        row = iota((block * span, 1), 0)
        dest = floordiv(row, span)
        j = row - dest * span
        plane = floordiv(j, CAP)
        slot = expert_of(first + dest, place_ref[3]) * CAP + j - plane * CAP
        main = rows_of(slot, plane).reshape(block, span, part)
        out_ref[:, source * span : (source + 1) * span] = main
        j = iota((span, 1), 0)
        plane = floordiv(j, CAP)
        extras.append(rows_of(experts * CAP + j - plane * CAP, plane))
    extra = jnp.concatenate(extras, 0)
    out_ref[:, 2 * span :] = jnp.broadcast_to(extra[None], (block, 2 * span, part))


def pack_scaled(place, raws, experts):
    part = raws[0].shape[-1]
    dests = experts // 2
    block = 8
    span = 4 * CAP
    return pl.pallas_call(
        functools.partial(pack_scaled_kernel, experts),
        grid_spec=pltpu.PrefetchScalarGridSpec(
            num_scalar_prefetch=1,
            grid=(dests // block,),
            in_specs=[pl.BlockSpec(r.shape, lambda g, s, n=r.ndim: (0,) * n) for r in raws],
            out_specs=pl.BlockSpec((block, 4 * span, part), lambda g, s: (g, 0, 0)),
        ),
        out_shape=jax.ShapeDtypeStruct((dests, 4 * span, part), BF16),
        compiler_params=pltpu.CompilerParams(vmem_limit_bytes=VMEM_LIMIT),
        name="pack_scaled",
    )(place, *raws)


def silu(v):
    return v / (1.0 + jnp.exp(-v))


def compact(senders):
    r, c = iota((senders * CAP, 1), 0), iota((senders * CAP, senders * 8), 1)
    src = floordiv(r, CAP)
    s = r - src * CAP
    return src, s, c, pick(c == src * 8 + s)


def hidden_main_kernel(x_ref, w_ref, out_ref, rows_ref):
    senders = x_ref.shape[0]
    width = w_ref.shape[0]
    part = width // 4
    head = 3 * part

    @pl.when(pl.program_id(0) == 0)
    def _():
        src, s, c, choose = compact(senders)
        for source in range(2):
            x = x_ref[:, :, source * head : (source + 1) * head].reshape(senders * 8, head)
            first = source * senders * CAP
            into = slice(first, first + senders * CAP)
            rows_ref[into, 0:head] = jnp.dot(choose, x, preferred_element_type=F32).astype(BF16)
            tail = jnp.zeros((senders * CAP, part), F32)
            for k in range(3):
                held = (s >= 2 * k) & (s < 2 * k + 2)
                mask = c == jnp.where(held, src * 8 + CAP + s - 2 * k, -1)
                tail = tail + jnp.dot(
                    pick(mask), x[:, k * part : (k + 1) * part], preferred_element_type=F32
                )
            rows_ref[into, head:] = tail.astype(BF16)

    v = jnp.dot(rows_ref[...], w_ref[...], preferred_element_type=F32)
    out_ref[...] = silu(v).astype(BF16)


def hidden_main(x, weight):
    senders = x.shape[0]
    width, hid = weight.shape
    count = 2 * senders * CAP
    block = 256
    return pl.pallas_call(
        hidden_main_kernel,
        grid=(hid // block,),
        in_specs=[
            pl.BlockSpec((senders, 8, 6 * width // 4), lambda n: (0, 0, 0)),
            pl.BlockSpec((width, block), lambda n: (0, n)),
        ],
        out_specs=pl.BlockSpec((count, block), lambda n: (0, n)),
        out_shape=jax.ShapeDtypeStruct((count, hid), BF16),
        scratch_shapes=[pltpu.VMEM((count, width), BF16)],
        compiler_params=pltpu.CompilerParams(vmem_limit_bytes=VMEM_LIMIT),
        name="hidden_main",
    )(x, weight)


def hidden_extra_kernel(place_ref, near_ref, far_ref, w_ref, out_ref, rows_ref):
    senders, _, width = near_ref.shape
    half = width // 2
    count = senders * CAP
    is_hot = place_ref[0] > 0

    @pl.when(is_hot & (pl.program_id(0) == 0))
    def _():
        choose = compact(senders)[-1]

        def put(x_ref, first):
            for source in range(2):
                x = x_ref[:, :, source * half : (source + 1) * half].reshape(senders * 8, half)
                rows = jnp.dot(choose, x, preferred_element_type=F32).astype(BF16)
                rows_ref[source * count : (source + 1) * count, first : first + half] = rows

        for core in range(2):

            @pl.when(place_ref[2] == core)
            def _():
                put(near_ref, core * half)
                put(far_ref, (1 - core) * half)

    @pl.when(is_hot)
    def _():
        v = jnp.dot(rows_ref[...], w_ref[...], preferred_element_type=F32)
        out_ref[...] = silu(v).astype(BF16)

    @pl.when(jnp.logical_not(is_hot))
    def _():
        out_ref[...] = jnp.zeros_like(out_ref)


def hidden_extra(place, near, far, weight):
    senders = near.shape[0]
    width, hid = weight.shape
    count = 2 * senders * CAP
    block = 256
    x_spec = pl.BlockSpec(near.shape, lambda n, s: (0, 0, 0))
    return pl.pallas_call(
        hidden_extra_kernel,
        grid_spec=pltpu.PrefetchScalarGridSpec(
            num_scalar_prefetch=1,
            grid=(hid // block,),
            in_specs=[x_spec, x_spec, pl.BlockSpec((width, block), lambda n, s: (0, n))],
            out_specs=pl.BlockSpec((count, block), lambda n, s: (0, n)),
            scratch_shapes=[pltpu.VMEM((count, width), BF16)],
        ),
        out_shape=jax.ShapeDtypeStruct((count, hid), BF16),
        compiler_params=pltpu.CompilerParams(vmem_limit_bytes=VMEM_LIMIT),
        name="hidden_extra",
    )(place, near, far, weight)


GROUP = 8


def by_plane(planes):
    n = GROUP * CAP
    rows = planes * 2 * n
    o = iota((rows, 1), 0)
    pair = floordiv(o, n)
    rest = o - pair * n
    plane, source = pair >> 1, pair & 1
    sender = floordiv(rest, CAP)
    origin = ((sender * 2 + source) * planes + plane) * CAP + rest - sender * CAP
    return pick(iota((rows, rows), 1) == origin)


def grad_kernel(place_ref, near_ref, far_ref, x0, x1, x2, x3, s_ref, sx_ref, out_ref, acc_ref):
    planes, _, _, hid = near_ref.shape
    part = s_ref.shape[-1]
    g = pl.program_id(0)

    choose = by_plane(planes)

    def ordered(s):
        s = s.reshape(planes * 2 * GROUP * CAP, part)
        return jnp.dot(choose, s, preferred_element_type=F32).astype(BF16)

    def total(hs, s):
        h = jnp.concatenate(hs, 0)
        return lax.dot_general(h, s, (((0,), (0,)), ((), ())), preferred_element_type=F32)

    sender = floordiv(iota((near_ref.shape[2], 1), 0), CAP)
    is_z = place_ref[3]
    even, odd = pick((sender & 1) == 0), pick((sender & 1) == 1)
    odd_z = [pick(((sender & 1) == 1) & (is_z == z)) for z in range(2)]

    def main():
        hs = []
        for d in range(planes):
            plane = place_ref[1] + planes - d
            other = lax.rem(plane + 1 - 2 * is_z, planes)
            plane = lax.rem(plane, planes)
            hs += [near_ref[plane, 0], far_ref[plane, 0] * even + far_ref[other, 0] * odd]
        return total(hs, ordered(s_ref[...]))

    @pl.when(g == 0)
    def _():
        acc_ref[...] = main()

    @pl.when(g > 0)
    def _():
        acc_ref[...] += main()

    @pl.when(place_ref[0] > 0)
    def _():
        xs = (x0, x1, x2, x3)
        hs = []
        for d in range(planes):
            other = xs[d - 1][1] * odd_z[0] + xs[(d + 1) % planes][1] * odd_z[1]
            hs += [xs[d][0], xs[d][1] * even + other]
        acc_ref[...] += total(hs, ordered(sx_ref[...]))

    @pl.when(g == pl.num_programs(0) - 1)
    def _():
        out_ref[...] = acc_ref[...].astype(out_ref.dtype)


def grad_of(place, hidden, extras, s):
    planes, _, hid = hidden.shape
    senders, span, part = s.shape
    n = GROUP * CAP
    hidden = hidden.reshape(planes, 2, -1, hid)
    h_specs = [pl.BlockSpec((planes, 1, n, hid), lambda g, s, i=i: (0, i, g, 0)) for i in range(2)]
    x_spec = pl.BlockSpec((2, n, hid), lambda g, s: (0, g, 0))
    s_specs = [pl.BlockSpec((GROUP, span // 2, part), lambda g, s, i=i: (g, i, 0)) for i in range(2)]
    return pl.pallas_call(
        grad_kernel,
        grid_spec=pltpu.PrefetchScalarGridSpec(
            num_scalar_prefetch=1,
            grid=(senders // GROUP,),
            in_specs=h_specs
            + [x_spec] * 4
            + s_specs,
            out_specs=pl.BlockSpec((hid, part), lambda g, s: (0, 0)),
            scratch_shapes=[pltpu.VMEM((hid, part), F32)],
        ),
        out_shape=jax.ShapeDtypeStruct((hid, part), BF16),
        compiler_params=pltpu.CompilerParams(vmem_limit_bytes=VMEM_LIMIT),
        name="grad_of",
    )(place, hidden, hidden, *[x.reshape(2, -1, hid) for x in extras], s, s)


def join_kernel(in_ref, out_ref):
    out_ref[...] = in_ref[...].astype(F32)


def join(parts):
    planes, rows, part = parts.shape
    return pl.pallas_call(
        join_kernel,
        grid=(planes,),
        in_specs=[pl.BlockSpec((1, rows, part), lambda n: (n, 0, 0))],
        out_specs=pl.BlockSpec((1, rows, part), lambda n: (0, 0, n)),
        out_shape=jax.ShapeDtypeStruct((1, rows, planes * part), F32),
        compiler_params=pltpu.CompilerParams(vmem_limit_bytes=VMEM_LIMIT),
        name="join",
    )(parts)


def bf16_parts(x):
    high = lax.reduce_precision(x, 8, 7)
    mid = lax.reduce_precision(x - high, 8, 7)
    return [high, mid, x - high - mid]


def z_neighbours(experts, planes):
    pairs = []
    for e in range(experts):
        step = 0 if e & 1 == 0 else (1 if (e >> 3) & 1 else -1)
        pairs += [(e * planes + p, (e ^ 8) * planes + (p + step) % planes) for p in range(planes)]
    return pairs


def local(tokens, cotangent, routes, gates, gate_weight):
    experts = lax.axis_size("expert")
    planes = lax.axis_size("dp")
    me = lax.axis_index("expert")
    dp = lax.axis_index("dp")
    core = me & 1
    other_z = [(i, i ^ 8) for i in range(experts)]
    other_core = [(i, i ^ 1) for i in range(experts)]
    same_z = [[i for i in range(experts) if (i >> 3) & 1 == z] for z in range(2)]

    route_rows = routes.T.astype(F32)
    gate_rows = gates.T
    meta = jnp.concatenate(
        [route_rows, jnp.stack(bf16_parts(gate_rows[0])), jnp.stack(bf16_parts(gate_rows[1]))], 0
    )
    named = (routes.reshape(-1)[:, None] == jnp.arange(experts, dtype=jnp.int32)[None, :]).astype(F32)
    hot_expert = jnp.argmax(jnp.sum(named, 0)).astype(jnp.int32)
    hot = (hot_expert == me).astype(jnp.int32)
    place = jnp.stack([hot, dp, core, (me >> 3) & 1]).astype(jnp.int32)

    def dispatch(x):
        return lax.all_to_all(x, "expert", 0, 0, tiled=True, axis_index_groups=same_z)

    weight = gate_weight[0]

    either_z = z_neighbours(experts, planes)
    far_tokens = lax.ppermute(tokens, ("expert", "dp"), either_z)
    far_meta = lax.ppermute(meta, ("expert", "dp"), either_z)
    blocks = split_raw(place, cotangent, meta)
    far_tokens, far_meta, blocks = lax.optimization_barrier((far_tokens, far_meta, blocks))
    sent = pack_tokens(place, (meta, far_meta), (tokens, far_tokens), experts)
    arrived = dispatch(sent)

    raw = [blocks[0]]
    for d in range(1, planes):
        raw.append(lax.ppermute(blocks[d], "dp", [(i, (i + d) % planes) for i in range(planes)]))
    far_own = lax.ppermute(blocks[0], "expert", other_z)
    far_own, raw = lax.optimization_barrier((far_own, raw))
    moved = jnp.stack(raw[1:])
    far_moved = lax.ppermute(moved, "expert", other_z)
    scaled = pack_scaled(place, (blocks[0], moved, far_own, far_moved), experts)
    arrived, scaled = lax.optimization_barrier((arrived, scaled))

    scaled = dispatch(scaled)

    hidden = hidden_main(arrived, weight)
    arrived, _ = lax.optimization_barrier((arrived, hidden))
    hidden = lax.all_gather(hidden, "dp")
    extra = arrived[:, :, 6 * arrived.shape[-1] // 10 :]
    far_extra = lax.ppermute(extra, "expert", other_core)
    own_extra = hidden_extra(place, extra, far_extra, weight)

    def share(z, c):
        def permutes(x):
            def shift(y, d):
                pairs = [
                    (e * planes + i, e * planes + (i + d) % planes)
                    for e in range(experts)
                    if (e >> 3) & 1 == z and e & 1 == c
                    for i in range(planes)
                ]
                return lax.ppermute(y, ("expert", "dp"), pairs)

            half = x.shape[0] // 2
            before, after = shift(x, 1), shift(x, -1)
            opposite = jnp.concatenate([shift(before[:half], 1), shift(after[half:], -1)], 0)
            return before, opposite, after

        return permutes

    table = [share(z, c) for z in range(2) for c in range(2)]
    extras = lax.switch(((hot_expert >> 3) & 1) * 2 + (hot_expert & 1), table, own_extra)

    scaled, own_extra, extras = lax.optimization_barrier((scaled, own_extra, extras))
    extras = (own_extra, *extras)
    grad = grad_of(place, hidden, extras, scaled)
    hid = grad.shape[0] // planes
    grad = lax.all_to_all(grad.reshape(planes, hid, -1), "dp", 0, 0, tiled=True)
    return join(grad)


def solution(mesh):
    placed = (
        P(("expert", "dp"), None),
        P(("expert", "dp"), None),
        P(("expert", "dp"), None),
        P(("expert", "dp"), None),
        P("expert", None, None),
    )
    return jax.shard_map(
        local, mesh=mesh, in_specs=placed, out_specs=P("expert", "dp", None), check_vma=False
    )
```

```python
import functools

import jax
import jax.numpy as jnp
from jax import lax
from jax.experimental import pallas as pl
from jax.experimental.pallas import tpu as pltpu
from jax.sharding import PartitionSpec as P

CAP = 6
F32 = jnp.float32
BF16 = jnp.bfloat16
VMEM_LIMIT = 56 * 1024 * 1024


def iota(shape, dim):
    return lax.broadcasted_iota(jnp.int32, shape, dim)


def floordiv(a, n):
    return jnp.floor((a.astype(F32) + 0.5) * (1.0 / n)).astype(jnp.int32)


def slot_ranks(route):
    tok = route.shape[1]
    column = route.T
    r0, r1 = route[0:1], route[1:2]
    c0, c1 = column[:, 0:1], column[:, 1:2]
    before = iota((tok, tok), 0) < iota((tok, tok), 1)

    def count(mask):
        return jnp.sum(jnp.where(mask, 1.0, 0.0), 0, keepdims=True)

    return count((c0 == r0) & before), count(c0 == r1) + count((c1 == r1) & before)


def slot_key(r, rank, experts):
    return jnp.where(rank < CAP, r * CAP + rank, experts * CAP + rank - CAP).astype(jnp.int32)


def slot_keys(route, experts):
    rank0, rank1 = slot_ranks(route)
    return slot_key(route[0:1], rank0, experts), slot_key(route[1:2], rank1, experts)


def split_raw_kernel(place_ref, q0_ref, q1_ref, q2_ref, q3_ref, meta_ref, *out_refs):
    tok, part = q0_ref.shape
    ranks = jnp.concatenate([*slot_ranks(meta_ref[...]), jnp.zeros((6, tok), F32)], 0)
    note = jnp.concatenate([meta_ref[...], ranks], 0).astype(BF16)
    note = jnp.concatenate([note, jnp.zeros((16, part - tok), BF16)], 1)
    for in_ref, out_ref in zip((q0_ref, q1_ref, q2_ref, q3_ref), out_refs):
        out_ref[0:tok, :] = in_ref[...]
        out_ref[tok:, :] = note


def split_raw(place, cotangent, meta):
    tok, width = cotangent.shape
    part = width // 4
    quarter = [pl.BlockSpec((tok, part), lambda i, s, d=d: (0, lax.rem(s[1] + d, 4))) for d in range(4)]
    return pl.pallas_call(
        split_raw_kernel,
        grid_spec=pltpu.PrefetchScalarGridSpec(
            num_scalar_prefetch=1,
            grid=(1,),
            in_specs=quarter + [pl.BlockSpec(meta.shape, lambda i, s: (0, 0))],
            out_specs=[pl.BlockSpec((tok + 16, part), lambda i, s: (0, 0))] * 4,
        ),
        out_shape=[jax.ShapeDtypeStruct((tok + 16, part), BF16)] * 4,
        compiler_params=pltpu.CompilerParams(vmem_limit_bytes=VMEM_LIMIT),
        name="split_raw",
    )(place, cotangent, cotangent, cotangent, cotangent, meta)


def pick(mask):
    return jnp.where(mask, 1.0, 0.0).astype(BF16)


def expert_of(dest, z):
    return (dest >> 3) * 16 + z * 8 + (dest & 7)


def fold_rows(place_ref, keys, tokens_ref, out_ref, begin):
    dests = out_ref.shape[0]
    part = tokens_ref.shape[1] // 4
    key0, key1 = keys
    row = iota((dests * 8, 1), 0)
    jj = row & 7
    first = expert_of(row >> 3, place_ref[3]) * CAP

    def choose(slot):
        return pick((slot == key0) | (slot == key1))

    head = choose(jnp.where(jj < CAP, first + jj, -1))
    for k in range(3):
        tail = choose(jnp.where(jj >= CAP, first + 2 * k + jj - CAP, -1))
        right = [tokens_ref[:, i * part : (i + 1) * part] for i in (k, 3)]
        left, right = jnp.concatenate([head, tail], 1), jnp.concatenate(right, 0)
        rows = jnp.dot(left, right, preferred_element_type=F32).astype(BF16)
        out_ref[:, :, begin + k * part : begin + (k + 1) * part] = rows.reshape(dests, 8, part)


def pack_tokens_kernel(experts, place_ref, a_meta, b_meta, a_ref, b_ref, out_ref):
    dests = out_ref.shape[0]
    width = a_ref.shape[1]
    half, head = width // 2, 3 * width // 4
    slot = experts * CAP + iota((8, 1), 0)
    odd = (iota((dests, 1, 1), 0) & 1) == 1
    for source, (meta, in_ref) in enumerate(((a_meta, a_ref), (b_meta, b_ref))):
        key0, key1 = slot_keys(meta[...], experts)
        fold_rows(place_ref, (key0, key1), in_ref, out_ref, source * head)
        left = pick((slot == key0) | (slot == key1))
        rows = jnp.dot(left, in_ref[...], preferred_element_type=F32)[None]
        first = 2 * head + source * half
        out_ref[:, :, first : first + half] = jnp.where(odd, rows[..., half:], rows[..., :half]).astype(BF16)


def pack_tokens(place, metas, tokens, experts):
    return pl.pallas_call(
        functools.partial(pack_tokens_kernel, experts),
        in_specs=[pl.BlockSpec(memory_space=pltpu.SMEM)] + [pl.BlockSpec(memory_space=pltpu.VMEM)] * 4,
        out_shape=jax.ShapeDtypeStruct((experts // 2, 8, 10 * tokens[0].shape[1] // 4), BF16),
        compiler_params=pltpu.CompilerParams(vmem_limit_bytes=VMEM_LIMIT),
        name="pack_tokens",
    )(place, *metas, *tokens)


def pack_scaled_kernel(experts, place_ref, own_ref, moved_ref, far_own_ref, far_moved_ref, out_ref):
    block, _, part = out_ref.shape
    extras = []
    tok = 128
    planes = 4
    span = planes * CAP
    first = pl.program_id(0) * block

    for source, (first_ref, others_ref) in enumerate(((own_ref, moved_ref), (far_own_ref, far_moved_ref))):
        raws = [first_ref[...]] + [others_ref[p] for p in range(planes - 1)]
        facts = []
        for p in range(planes):
            meta = raws[p][tok : tok + 16, 0:tok].astype(F32)
            gate0 = (meta[2:3] + meta[3:4]) + meta[4:5]
            gate1 = (meta[5:6] + meta[6:7]) + meta[7:8]
            keys = [slot_key(meta[i : i + 1], meta[8 + i : 9 + i], experts) for i in range(2)]
            facts.append((*keys, gate0, gate1))
        right = jnp.concatenate([raw[0:tok, :] for raw in raws], 0)

        def rows_of(slot, plane):
            lefts = []
            gate = jnp.zeros(slot.shape, F32)
            for p, (key0, key1, gate0, gate1) in enumerate(facts):
                mine = jnp.where(plane == p, slot, -1)
                hit0, hit1 = mine == key0, mine == key1
                both = jnp.where(hit0, gate0, 0.0) + jnp.where(hit1, gate1, 0.0)
                gate = gate + jnp.sum(both, 1, keepdims=True)
                lefts.append(pick(hit0 | hit1))
            rows = jnp.dot(jnp.concatenate(lefts, 1), right, preferred_element_type=F32)
            return (gate * rows).astype(BF16)

        row = iota((block * span, 1), 0)
        dest = floordiv(row, span)
        j = row - dest * span
        plane = floordiv(j, CAP)
        slot = expert_of(first + dest, place_ref[3]) * CAP + j - plane * CAP
        main = rows_of(slot, plane).reshape(block, span, part)
        out_ref[:, source * span : (source + 1) * span] = main
        j = iota((span, 1), 0)
        plane = floordiv(j, CAP)
        extras.append(rows_of(experts * CAP + j - plane * CAP, plane))
    extra = jnp.concatenate(extras, 0)
    out_ref[:, 2 * span :] = jnp.broadcast_to(extra[None], (block, 2 * span, part))


def pack_scaled(place, raws, experts):
    part = raws[0].shape[-1]
    dests = experts // 2
    block = 8
    span = 4 * CAP
    return pl.pallas_call(
        functools.partial(pack_scaled_kernel, experts),
        grid_spec=pltpu.PrefetchScalarGridSpec(
            num_scalar_prefetch=1,
            grid=(dests // block,),
            in_specs=[pl.BlockSpec(r.shape, lambda g, s, n=r.ndim: (0,) * n) for r in raws],
            out_specs=pl.BlockSpec((block, 4 * span, part), lambda g, s: (g, 0, 0)),
        ),
        out_shape=jax.ShapeDtypeStruct((dests, 4 * span, part), BF16),
        compiler_params=pltpu.CompilerParams(vmem_limit_bytes=VMEM_LIMIT),
        name="pack_scaled",
    )(place, *raws)


def silu(v):
    return v / (1.0 + jnp.exp(-v))


def compact(senders):
    r, c = iota((senders * CAP, 1), 0), iota((senders * CAP, senders * 8), 1)
    src = floordiv(r, CAP)
    s = r - src * CAP
    return src, s, c, pick(c == src * 8 + s)


def hidden_main_kernel(x_ref, w_ref, out_ref, rows_ref):
    senders = x_ref.shape[0]
    width = w_ref.shape[0]
    part = width // 4
    head = 3 * part

    @pl.when(pl.program_id(0) == 0)
    def _():
        src, s, c, choose = compact(senders)
        for source in range(2):
            x = x_ref[:, :, source * head : (source + 1) * head].reshape(senders * 8, head)
            first = source * senders * CAP
            into = slice(first, first + senders * CAP)
            rows_ref[into, 0:head] = jnp.dot(choose, x, preferred_element_type=F32).astype(BF16)
            tail = jnp.zeros((senders * CAP, part), F32)
            for k in range(3):
                held = (s >= 2 * k) & (s < 2 * k + 2)
                mask = c == jnp.where(held, src * 8 + CAP + s - 2 * k, -1)
                tail = tail + jnp.dot(
                    pick(mask), x[:, k * part : (k + 1) * part], preferred_element_type=F32
                )
            rows_ref[into, head:] = tail.astype(BF16)

    v = jnp.dot(rows_ref[...], w_ref[...], preferred_element_type=F32)
    out_ref[...] = silu(v).astype(BF16)


def hidden_main(x, weight):
    senders = x.shape[0]
    width, hid = weight.shape
    count = 2 * senders * CAP
    block = 256
    return pl.pallas_call(
        hidden_main_kernel,
        grid=(hid // block,),
        in_specs=[
            pl.BlockSpec((senders, 8, 6 * width // 4), lambda n: (0, 0, 0)),
            pl.BlockSpec((width, block), lambda n: (0, n)),
        ],
        out_specs=pl.BlockSpec((count, block), lambda n: (0, n)),
        out_shape=jax.ShapeDtypeStruct((count, hid), BF16),
        scratch_shapes=[pltpu.VMEM((count, width), BF16)],
        compiler_params=pltpu.CompilerParams(vmem_limit_bytes=VMEM_LIMIT),
        name="hidden_main",
    )(x, weight)


def hidden_extra_kernel(place_ref, near_ref, far_ref, w_ref, out_ref, rows_ref):
    senders, _, width = near_ref.shape
    half = width // 2
    count = senders * CAP
    is_hot = place_ref[0] > 0

    @pl.when(is_hot & (pl.program_id(0) == 0))
    def _():
        choose = compact(senders)[-1]

        def put(x_ref, first):
            for source in range(2):
                x = x_ref[:, :, source * half : (source + 1) * half].reshape(senders * 8, half)
                rows = jnp.dot(choose, x, preferred_element_type=F32).astype(BF16)
                rows_ref[source * count : (source + 1) * count, first : first + half] = rows

        for core in range(2):

            @pl.when(place_ref[2] == core)
            def _():
                put(near_ref, core * half)
                put(far_ref, (1 - core) * half)

    @pl.when(is_hot)
    def _():
        v = jnp.dot(rows_ref[...], w_ref[...], preferred_element_type=F32)
        out_ref[...] = silu(v).astype(BF16)

    @pl.when(jnp.logical_not(is_hot))
    def _():
        out_ref[...] = jnp.zeros_like(out_ref)


def hidden_extra(place, near, far, weight):
    senders = near.shape[0]
    width, hid = weight.shape
    count = 2 * senders * CAP
    block = 256
    x_spec = pl.BlockSpec(near.shape, lambda n, s: (0, 0, 0))
    return pl.pallas_call(
        hidden_extra_kernel,
        grid_spec=pltpu.PrefetchScalarGridSpec(
            num_scalar_prefetch=1,
            grid=(hid // block,),
            in_specs=[x_spec, x_spec, pl.BlockSpec((width, block), lambda n, s: (0, n))],
            out_specs=pl.BlockSpec((count, block), lambda n, s: (0, n)),
            scratch_shapes=[pltpu.VMEM((count, width), BF16)],
        ),
        out_shape=jax.ShapeDtypeStruct((count, hid), BF16),
        compiler_params=pltpu.CompilerParams(vmem_limit_bytes=VMEM_LIMIT),
        name="hidden_extra",
    )(place, near, far, weight)


GROUP = 8


def by_plane(planes):
    n = GROUP * CAP
    rows = planes * 2 * n
    o = iota((rows, 1), 0)
    pair = floordiv(o, n)
    rest = o - pair * n
    plane, source = pair >> 1, pair & 1
    sender = floordiv(rest, CAP)
    origin = ((sender * 2 + source) * planes + plane) * CAP + rest - sender * CAP
    return pick(iota((rows, rows), 1) == origin)


def grad_kernel(place_ref, near_ref, far_ref, x0, x1, x2, x3, s_ref, sx_ref, out_ref, acc_ref):
    planes, _, _, hid = near_ref.shape
    part = s_ref.shape[-1]
    g = pl.program_id(0)

    choose = by_plane(planes)

    def ordered(s):
        s = s.reshape(planes * 2 * GROUP * CAP, part)
        return jnp.dot(choose, s, preferred_element_type=F32).astype(BF16)

    def total(hs, s):
        h = jnp.concatenate(hs, 0)
        return lax.dot_general(h, s, (((0,), (0,)), ((), ())), preferred_element_type=F32)

    sender = floordiv(iota((near_ref.shape[2], 1), 0), CAP)
    is_z = place_ref[3]
    even, odd = pick((sender & 1) == 0), pick((sender & 1) == 1)
    odd_z = [pick(((sender & 1) == 1) & (is_z == z)) for z in range(2)]

    def main():
        hs = []
        for d in range(planes):
            plane = place_ref[1] + planes - d
            other = lax.rem(plane + 1 - 2 * is_z, planes)
            plane = lax.rem(plane, planes)
            hs += [near_ref[plane, 0], far_ref[plane, 0] * even + far_ref[other, 0] * odd]
        return total(hs, ordered(s_ref[...]))

    @pl.when(g == 0)
    def _():
        acc_ref[...] = main()

    @pl.when(g > 0)
    def _():
        acc_ref[...] += main()

    @pl.when(place_ref[0] > 0)
    def _():
        xs = (x0, x1, x2, x3)
        hs = []
        for d in range(planes):
            other = xs[d - 1][1] * odd_z[0] + xs[(d + 1) % planes][1] * odd_z[1]
            hs += [xs[d][0], xs[d][1] * even + other]
        acc_ref[...] += total(hs, ordered(sx_ref[...]))

    @pl.when(g == pl.num_programs(0) - 1)
    def _():
        out_ref[...] = acc_ref[...].astype(out_ref.dtype)


def grad_of(place, hidden, extras, s):
    planes, _, hid = hidden.shape
    senders, span, part = s.shape
    n = GROUP * CAP
    hidden = hidden.reshape(planes, 2, -1, hid)
    h_specs = [pl.BlockSpec((planes, 1, n, hid), lambda g, s, i=i: (0, i, g, 0)) for i in range(2)]
    x_spec = pl.BlockSpec((2, n, hid), lambda g, s: (0, g, 0))
    s_specs = [pl.BlockSpec((GROUP, span // 2, part), lambda g, s, i=i: (g, i, 0)) for i in range(2)]
    return pl.pallas_call(
        grad_kernel,
        grid_spec=pltpu.PrefetchScalarGridSpec(
            num_scalar_prefetch=1,
            grid=(senders // GROUP,),
            in_specs=h_specs
            + [x_spec] * 4
            + s_specs,
            out_specs=pl.BlockSpec((hid, part), lambda g, s: (0, 0)),
            scratch_shapes=[pltpu.VMEM((hid, part), F32)],
        ),
        out_shape=jax.ShapeDtypeStruct((hid, part), BF16),
        compiler_params=pltpu.CompilerParams(vmem_limit_bytes=VMEM_LIMIT),
        name="grad_of",
    )(place, hidden, hidden, *[x.reshape(2, -1, hid) for x in extras], s, s)


def join_kernel(in_ref, out_ref):
    out_ref[...] = in_ref[...].astype(F32)


def join(parts):
    planes, rows, part = parts.shape
    return pl.pallas_call(
        join_kernel,
        grid=(planes, 2),
        in_specs=[pl.BlockSpec((1, rows // 2, part), lambda n, h: (n, h, 0))],
        out_specs=pl.BlockSpec((1, rows // 2, part), lambda n, h: (0, h, n)),
        out_shape=jax.ShapeDtypeStruct((1, rows, planes * part), F32),
        compiler_params=pltpu.CompilerParams(vmem_limit_bytes=VMEM_LIMIT),
        name="join",
    )(parts)


def bf16_parts(x):
    high = lax.reduce_precision(x, 8, 7)
    mid = lax.reduce_precision(x - high, 8, 7)
    return [high, mid, x - high - mid]


def z_neighbours(experts, planes):
    pairs = []
    for e in range(experts):
        step = 0 if e & 1 == 0 else (1 if (e >> 3) & 1 else -1)
        pairs += [(e * planes + p, (e ^ 8) * planes + (p + step) % planes) for p in range(planes)]
    return pairs


def local(tokens, cotangent, routes, gates, gate_weight):
    experts = lax.axis_size("expert")
    planes = lax.axis_size("dp")
    me = lax.axis_index("expert")
    dp = lax.axis_index("dp")
    core = me & 1
    other_z = [(i, i ^ 8) for i in range(experts)]
    other_core = [(i, i ^ 1) for i in range(experts)]
    same_z = [[i for i in range(experts) if (i >> 3) & 1 == z] for z in range(2)]

    route_rows = routes.T.astype(F32)
    gate_rows = gates.T
    meta = jnp.concatenate(
        [route_rows, jnp.stack(bf16_parts(gate_rows[0])), jnp.stack(bf16_parts(gate_rows[1]))], 0
    )
    named = (routes.reshape(-1)[:, None] == jnp.arange(experts, dtype=jnp.int32)[None, :]).astype(F32)
    hot_expert = jnp.argmax(jnp.sum(named, 0)).astype(jnp.int32)
    hot = (hot_expert == me).astype(jnp.int32)
    place = jnp.stack([hot, dp, core, (me >> 3) & 1]).astype(jnp.int32)

    def dispatch(x):
        return lax.all_to_all(x, "expert", 0, 0, tiled=True, axis_index_groups=same_z)

    weight = gate_weight[0]

    either_z = z_neighbours(experts, planes)
    far_tokens = lax.ppermute(tokens, ("expert", "dp"), either_z)
    far_meta = lax.ppermute(meta, ("expert", "dp"), either_z)
    blocks = split_raw(place, cotangent, meta)
    far_tokens, far_meta, blocks = lax.optimization_barrier((far_tokens, far_meta, blocks))
    sent = pack_tokens(place, (meta, far_meta), (tokens, far_tokens), experts)
    arrived = dispatch(sent)

    raw = [blocks[0]]
    for d in range(1, planes):
        raw.append(lax.ppermute(blocks[d], "dp", [(i, (i + d) % planes) for i in range(planes)]))
    far_own = lax.ppermute(blocks[0], "expert", other_z)
    far_own, raw = lax.optimization_barrier((far_own, raw))
    moved = jnp.stack(raw[1:])
    far_moved = lax.ppermute(moved, "expert", other_z)
    scaled = pack_scaled(place, (blocks[0], moved, far_own, far_moved), experts)
    arrived, scaled = lax.optimization_barrier((arrived, scaled))

    scaled = dispatch(scaled)

    hidden = hidden_main(arrived, weight)
    arrived, _ = lax.optimization_barrier((arrived, hidden))
    hidden = lax.all_gather(hidden, "dp")
    extra = arrived[:, :, 6 * arrived.shape[-1] // 10 :]
    far_extra = lax.ppermute(extra, "expert", other_core)
    own_extra = hidden_extra(place, extra, far_extra, weight)

    def share(z, c):
        def permutes(x):
            def shift(y, d):
                pairs = [
                    (e * planes + i, e * planes + (i + d) % planes)
                    for e in range(experts)
                    if (e >> 3) & 1 == z and e & 1 == c
                    for i in range(planes)
                ]
                return lax.ppermute(y, ("expert", "dp"), pairs)

            half = x.shape[0] // 2
            before, after = shift(x, 1), shift(x, -1)
            opposite = jnp.concatenate([shift(before[:half], 1), shift(after[half:], -1)], 0)
            return before, opposite, after

        return permutes

    table = [share(z, c) for z in range(2) for c in range(2)]
    extras = lax.switch(((hot_expert >> 3) & 1) * 2 + (hot_expert & 1), table, own_extra)

    scaled, own_extra, extras = lax.optimization_barrier((scaled, own_extra, extras))
    extras = (own_extra, *extras)
    grad = grad_of(place, hidden, extras, scaled)
    hid = grad.shape[0] // planes
    grad = lax.all_to_all(grad.reshape(planes, hid, -1), "dp", 0, 0, tiled=True)
    return join(grad)


def solution(mesh):
    placed = (
        P(("expert", "dp"), None),
        P(("expert", "dp"), None),
        P(("expert", "dp"), None),
        P(("expert", "dp"), None),
        P("expert", None, None),
    )
    return jax.shard_map(
        local, mesh=mesh, in_specs=placed, out_specs=P("expert", "dp", None), check_vma=False
    )
```
